32 devices in a mesh: grp: 2 (over y), ka: 16 (over z, x, core).
Axes of the slice: x: 2, y: 2, z: 4, core: 2. Of those that a mesh axis runs over, the one named last changes fastest.
Arguments:
- eigvecs: bfloat16 [16, 2, 64, 1024], P('ka'), may hold values from -0.25 to 0.25
- eigvals: bfloat16 [496, 2, 512], P('ka'), may hold values from -2 to 2
- kpoints: bfloat16 [3, 496], P(None, 'ka'), may hold values from 0 to 1
- counts: int32 [16], P('ka'), may hold values from 1 to 31, as said below
- energy_real: float32 [2], P('grp'), parts along dimension 0, may hold values from -0.5 to 0.5
- energy_imag: float32 [2], P('grp'), parts along dimension 0, may hold values from 0.1 to 0.4
- offsets: int32 [3, 16], replicated, may hold values from -4 to 4, as said below
- atom_orbitals: int32 [8], replicated, may hold values from 1 to 12, 64 in all
- positions: float32 [3, 8], replicated, may hold values from 0 to 1
- exch_split: float32 [64, 64], replicated, may hold values from -6 to 6
Outputs:
- exchange: float32 [32, 8, 8], P(('grp', 'ka')), parts along dimension 0
The draws below stay inside these ranges and needn't reach their ends.
There are 2 independent parts, one for each index of `grp`. The reference program is written for one: setup_inputs(seed, part) draws one part's arguments, and reference() takes and returns one part's arrays. A program takes and returns all parts, laid end to end along the dimension named above; an argument that names none is the same for every part. Nothing has to cross between parts.
Inputs may be any that keep to these rules, and one draw needn't show every extreme that they name: For every device d below the axis's middle, counts[d] + counts[d + 8] is at most 32, one of the two exceeds 16, and the pair of device 0 reaches the maximum count. `offsets`: for r < 8, column r + 8 is minus column r, and the first component of column r is 1 to 4.
All inputs are finite; a program needn't handle non-finite values.
Results may differ from the reference program's by a relative error of at most 0.0063.
The reference program's roundings to bfloat16 on the way count: a program that leaves them out, or rounds other values in their place, can miss the bound.
Values may be sent and summed in bfloat16 or wider, within the bound.
A program may use at most 128 MiB of HBM per device.

```python
import math
import jax
import jax.numpy as jnp
import numpy as np
from jax import lax

NORB = 512
MO = 64
NA = 8
MOST = 12
R_DEV = 1
KB = 16
KTOT = 496
N_KA = 16


def draw_counts(key, part):
    half_axis = N_KA // 2
    first_key, second_key, third_key = jax.random.split(jax.random.fold_in(key, 11), 3)
    busy_count = jax.random.randint(first_key, (half_axis,), KB + 1, 2 * KB)
    busy_count = busy_count.at[0].set(2 * KB - 1)
    spare_room = 2 * KB - busy_count
    drawn_count = 1 + jax.random.randint(second_key, (half_axis,), 0, 1 << 20) % spare_room
    which_first = jax.random.randint(third_key, (half_axis,), 0, 2)
    first_half = jnp.where(which_first == 1, busy_count, drawn_count)
    second = jnp.where(which_first == 1, drawn_count, busy_count)
    return jnp.concatenate([first_half, second]).astype(jnp.int32)


def draw_offsets(key, part):
    half_rows = R_DEV * N_KA // 2
    first_key, second_key = jax.random.split(jax.random.fold_in(key, 23), 2)
    leading = jax.random.randint(first_key, (1, half_rows), 1, 5)
    others = jax.random.randint(second_key, (2, half_rows), -4, 5)
    front = jnp.concatenate([leading, others], 0)
    return jnp.concatenate([front, -front], 1).astype(jnp.int32)


def block_scale(own_key, extent, cuts, smallest, high):
    gain, own = 1.0, jax.random.fold_in(own_key, 6)
    for axis_at, shards_of in cuts:
        steps = jnp.exp(jax.random.uniform(jax.random.fold_in(own, axis_at), (shards_of,), jnp.float32, smallest / len(cuts), high / len(cuts)))
        gain = gain * jnp.repeat(steps, extent[axis_at] // shards_of).reshape([-1 if axis == axis_at else 1 for axis in range(len(extent))])
    return gain


def profile(number_of, total, most, lean):
    portions = [(1 << 20) // math.isqrt(rank ** lean) + 1 for rank in range(2, number_of + 1)]
    rest, given = total - most - (number_of - 1), [1] * (number_of - 1)
    while rest > 0:
        candidates = [i for i in range(number_of - 1) if given[i] < most]
        pool, left = sum([portions[i] for i in candidates]), rest
        for i in candidates:
            extra = min(most - given[i], max(1, left * portions[i] // pool), rest)
            given[i] = given[i] + extra
            rest = rest - extra
    return np.array([most] + given)


def uneven(rng, count, total, limit, slope):
    if count == 2:
        one = jax.random.randint(rng, (), max(1, total - limit), min(limit, total - 1) + 1)
        return jnp.stack([one, total - one])
    lengths = jnp.asarray(profile(count, total, limit, slope), jnp.int32)
    twos = (count - 1) // 2
    donor, receiver = lengths[1:1 + 2 * twos:2], lengths[2:2 + 2 * twos:2]
    room = jnp.minimum(donor - 1, limit - receiver)
    moved = jax.random.randint(jax.random.fold_in(rng, 1), (twos,), 0, 1 << 20) % (room + 1)
    lengths = lengths.at[1:1 + 2 * twos:2].set(donor - moved).at[2:2 + 2 * twos:2].set(receiver + moved)
    return lengths[jax.random.permutation(jax.random.fold_in(rng, 2), count)]


def bell_draw(stream_key, extent, deviation, limit, cuts=(), kind=jnp.bfloat16):
    result = jax.random.normal(stream_key, extent, jnp.float32) * deviation
    if len(cuts) > 0:
        result = block_scale(stream_key, extent, cuts, -0.22, 0.18) * result
    return jnp.clip(result, min=-limit, max=limit).astype(kind)


def setup_inputs(seed: int = 0, part: int = 0) -> dict:
    splits = jax.random.split(jax.random.key(seed), 11)
    own_keys = jax.random.split(jax.random.fold_in(splits[10], part), 11)
    eigvecs = bell_draw(splits[0], (N_KA, 2, MO, 2 * NORB), NORB ** -0.5, 0.25, ((0, 16),))
    eigvals = jnp.clip(jax.random.uniform(splits[1], (KTOT, 2, NORB), jnp.float32, -2.0, 2.0) * block_scale(splits[1], (KTOT, 2, NORB), ((0, 16),), -0.4, 0.0), -2.0, 2.0).astype(jnp.bfloat16)
    kpoints = jnp.clip(1.0 * jax.random.uniform(splits[2], (3, KTOT), jnp.float32) ** block_scale(splits[2], (3, KTOT), ((1, 16),), -0.2, 0.2), 0.0, 1.0).astype(jnp.bfloat16)
    counts = draw_counts(jax.random.fold_in(splits[10], 71), part)
    energy_real = jnp.clip(jax.random.uniform(own_keys[4], (1,), jnp.float32, -0.5, 0.5), -0.5, 0.5)
    energy_imag = jnp.clip(jax.random.uniform(own_keys[5], (1,), jnp.float32, 0.1, 0.4), 0.1, 0.4)
    offsets = draw_offsets(jax.random.fold_in(splits[10], 71), part)
    atom_orbitals = uneven(splits[7], NA, MO, MOST, 0).astype(jnp.int32)
    positions = jnp.clip(jax.random.uniform(splits[8], (3, NA), jnp.float32, 0.0, 1.0), 0.0, 1.0)
    exch_split = bell_draw(splits[9], (MO, MO), 1.0, 6.0, (), jnp.float32)
    return {"eigvecs": eigvecs, "eigvals": eigvals, "kpoints": kpoints, "counts": counts, "energy_real": energy_real, "energy_imag": energy_imag, "offsets": offsets, "atom_orbitals": atom_orbitals, "positions": positions, "exch_split": exch_split}


inv_four_pi = 0.25 / 3.141592653589793
two_pi = 2.0 * 3.141592653589793


def member_table(atom_orbitals, mag):
    ends = jnp.cumsum(atom_orbitals)
    starts = ends - atom_orbitals
    orbital = jnp.arange(mag, dtype=jnp.int32)[:, None]
    return ((orbital >= starts[None, :]) & (orbital < ends[None, :])).astype(jnp.float32)


def bare_green(vectors, levels, energy_real, energy_imag):
    norb = levels.shape[-1]
    levels_wide = levels.astype(jnp.float32)
    shift = energy_real[0] - levels_wide
    denom = shift * shift + energy_imag[0] * energy_imag[0]
    real_factor = (shift / denom)[:, :, None, :]
    imag_factor = (-energy_imag[0] / denom)[:, :, None, :]
    wide = vectors.astype(jnp.float32)
    re_vec = wide[..., :norb]
    im_vec = wide[..., norb:]
    scaled = jnp.concatenate([re_vec * real_factor - im_vec * imag_factor,
                              re_vec * imag_factor + im_vec * real_factor], -1).astype(jnp.bfloat16)
    right = jnp.concatenate([vectors, jnp.concatenate([-vectors[..., norb:], vectors[..., :norb]], -1)], axis=-2)
    return jnp.einsum('ksan,scn->ksac', scaled.astype(jnp.float32), right.astype(jnp.float32),
                      precision=lax.Precision.HIGHEST)


def apply_gauge(product, coords, site):
    mag = site.shape[1]
    kpos = jnp.einsum('xk,xa->ka', coords.astype(jnp.float32), site, precision=lax.Precision.HIGHEST)
    phase = two_pi * (kpos[:, None, :] - kpos[:, :, None])
    cos_phase = jnp.cos(phase)[:, None]
    sin_phase = jnp.sin(phase)[:, None]
    green_re = product[..., :mag]
    green_im = product[..., mag:]
    new_re = green_re * cos_phase - green_im * sin_phase
    new_im = green_re * sin_phase + green_im * cos_phase
    stacked = jnp.stack([new_re, new_im], axis=2)
    return stacked.reshape(product.shape[0], 2, 2, mag * mag).astype(jnp.bfloat16)


def phase_terms(coords, slot_weights, lattice, grid, blocks):
    angle = two_pi * jnp.einsum('ck,cr->rk', coords.astype(jnp.float32), lattice.astype(jnp.float32),
                                precision=lax.Precision.HIGHEST)
    weight_wide = slot_weights.astype(jnp.float32)[None, :]
    cos_weight = (jnp.cos(angle) * weight_wide).astype(jnp.bfloat16)
    sin_weight = (jnp.sin(angle) * weight_wide).astype(jnp.bfloat16)

    def matmul(left, right):
        return jnp.dot(left, right, preferred_element_type=jnp.float32)

    def combine(sign, spin):
        real_sum = matmul(cos_weight, grid[:, spin, 0]) + sign * matmul(sin_weight, grid[:, spin, 1])
        imag_sum = matmul(cos_weight, grid[:, spin, 1]) - sign * matmul(sin_weight, grid[:, spin, 0])
        return [real_sum, imag_sum]

    pieces = combine(1.0, 0) + combine(1.0, 1)
    if blocks == 3:
        pieces = pieces + combine(-1.0, 1)
    return jnp.concatenate(pieces, axis=1)


def pair_exchange(up_block, down_block, exch_split, atom_orbitals):
    mag = exch_split.shape[0]
    rows = up_block.shape[0]
    area = mag * mag
    up_re = up_block[:, :area].reshape(rows, mag, mag)
    up_im = up_block[:, area:].reshape(rows, mag, mag)
    down_re = down_block[:, :area].reshape(rows, mag, mag)
    down_im = down_block[:, area:].reshape(rows, mag, mag)
    member = member_table(atom_orbitals, mag)
    same_atom = jnp.dot(member, member.T, precision=lax.Precision.HIGHEST)
    splitting = 0.5 * (exch_split + exch_split.T) * same_atom
    high = lax.Precision.HIGHEST
    left_re = jnp.einsum('ab,rbc->rac', splitting, up_re, precision=high)
    left_im = jnp.einsum('ab,rbc->rac', splitting, up_im, precision=high)
    right_re = jnp.einsum('ab,rbc->rac', splitting, down_re, precision=high)
    right_im = jnp.einsum('ab,rbc->rac', splitting, down_im, precision=high)
    im_part = left_re * jnp.swapaxes(right_im, 1, 2) + left_im * jnp.swapaxes(right_re, 1, 2)
    return -inv_four_pi * jnp.einsum('ai,rab,bj->rij', member, im_part, member, precision=high)


def reference(eigvecs, eigvals, kpoints, counts, energy_real, energy_imag, offsets, atom_orbitals, positions,
              exch_split):
    batches = counts.shape[0]
    kslot = eigvals.shape[0] // batches
    mag = eigvecs.shape[2]
    norb = eigvals.shape[2]
    area = mag * mag
    slot_index = jnp.arange(kslot, dtype=jnp.int32)
    inverse = (1.0 / counts.astype(jnp.float32)).astype(jnp.bfloat16)
    weights = jnp.where(slot_index[None, :] < counts[:, None], inverse[:, None],
                        jnp.zeros((), jnp.bfloat16))
    member = member_table(atom_orbitals, mag)
    site = jnp.dot(positions, member.T, precision=lax.Precision.HIGHEST)
    level_blocks = eigvals.reshape(batches, kslot, 2, norb)
    coord_blocks = jnp.transpose(kpoints.reshape(3, batches, kslot), (1, 0, 2))

    def step(total, batch):
        vectors, levels, coords, slot_weights = batch
        grid = apply_gauge(bare_green(vectors, levels, energy_real, energy_imag), coords, site)
        return total + phase_terms(coords, slot_weights, offsets, grid, 3), None

    start = jnp.zeros((offsets.shape[1], 6 * area), jnp.float32)
    terms, unused = lax.scan(step, start, (eigvecs, level_blocks, coord_blocks, weights))
    return pair_exchange(terms[:, :2 * area], terms[:, 4 * area:], exch_split, atom_orbitals)
```

```python
import functools

import jax
import jax.numpy as jnp
from jax import lax
from jax.experimental import pallas as pl
from jax.experimental.pallas import tpu as pltpu
from jax.sharding import PartitionSpec as P

inv_four_pi = 0.25 / 3.141592653589793
two_pi = 2.0 * 3.141592653589793

ROWS = 16
HIGH = lax.Precision.HIGHEST
ACROSS = (((1,), (1,)), ((), ()))


def wave(turns):
    part = (turns - jnp.round(turns)) * two_pi
    return jnp.cos(part), jnp.sin(part)


def one_hot(condition):
    return jnp.where(condition, 1.0, 0.0).astype(jnp.bfloat16)


def iota(shape, axis):
    return lax.broadcasted_iota(jnp.int32, shape, axis)


def kernel(
    n,
    vec_ref,
    lev_ref,
    k_ref,
    count_ref,
    er_ref,
    ei_ref,
    off_ref,
    orb_ref,
    pos_ref,
    split_ref,
    out_ref,
    vf,
    right,
    levels,
    fre,
    fim,
    ctab,
    stab,
    wbd,
    scaled,
    acc,
    acc2,
    acc3,
    send1,
    recv1,
    send2,
    recv2,
    send3,
    recv3,
    ssem1,
    rsem1,
    ssem2,
    rsem2,
    ssem3,
    rsem3,
):
    mag, norb = vec_ref.shape[2], vec_ref.shape[3] // 2
    kslot = lev_ref.shape[0]
    slots = levels.shape[1]
    atoms = orb_ref.shape[0]
    blocks = mag // ROWS
    chunks = 2 * blocks
    quarter, eighth = n // 4, n // 8
    wide = 2 * mag

    me = lax.axis_index("ka")
    b0, b1, q = lax.rem(me, 2), lax.rem(me // 2, 2), me // 4
    mate0 = {"ka": me + 1 - 2 * b0}
    mate1 = {"ka": me + 2 - 4 * b1}

    def peer(k):
        return lax.rem(q + k, quarter)

    def peer_id(k):
        return {"ka": peer(k) * 4 + b1 * 2 + b0}

    barrier = pltpu.get_barrier_semaphore()
    for other in [mate0, mate1] + [peer_id(k) for k in range(1, quarter)]:
        pl.semaphore_signal(
            barrier, inc=1, device_id=other, device_id_type=pl.DeviceIdType.MESH
        )

    for spin in range(2):
        vectors = vec_ref[0, spin]
        vf[spin] = vectors.astype(jnp.float32)
        right[spin, :mag, :] = vectors
        right[spin, mag:, :norb] = -vectors[:, norb:]
        right[spin, mag:, norb:] = vectors[:, :norb]
        levels[spin] = jnp.zeros((slots, norb), jnp.float32)
    for s in range(kslot):
        row = lev_ref[s].astype(jnp.float32)
        levels[0, s : s + 1, :] = row[0:1]
        levels[1, s : s + 1, :] = row[1:2]
    er, ei = er_ref[0], ei_ref[0]
    for spin in range(2):
        shift = er - levels[spin]
        denom = shift * shift + ei * ei
        inverse = 1.0 / denom
        fre[spin] = shift * inverse
        fim[spin] = -ei * inverse

    lane = iota((1, wide), 1)
    lane = jnp.where(lane >= mag, lane - mag, lane)
    down_rows = iota((mag, 1), 0)
    id_row = jnp.zeros((1, wide), jnp.int32)
    id_col = jnp.zeros((mag, 1), jnp.int32)
    end = jnp.int32(0)
    for i in range(atoms):
        end = end + orb_ref[i]
        id_row = id_row + jnp.where(lane >= end, 1, 0)
        id_col = id_col + jnp.where(down_rows >= end, 1, 0)

    coords = k_ref[...]
    eye = one_hot(iota((slots, kslot), 0) == iota((slots, kslot), 1))
    k_cols = lax.dot_general(eye, coords, ACROSS, preferred_element_type=jnp.float32)
    kpos = jnp.zeros((slots, wide), jnp.float32)
    for x in range(3):
        site = jnp.zeros((1, wide), jnp.float32)
        for i in range(atoms):
            site = jnp.where(id_row == i, pos_ref[x, i], site)
        kpos = kpos + k_cols[:, x : x + 1] * site
    cos_c, sin_c = wave(kpos)
    sign = jnp.where(iota((1, wide), 1) < mag, -1.0, 1.0)
    cos_s, sin_s = cos_c * sign, sin_c * sign
    for a in range(mag):
        cos_a, sin_a = cos_c[:, a : a + 1], sin_c[:, a : a + 1]
        ctab[a * slots : (a + 1) * slots, :] = cos_c * cos_a + sin_c * sin_a
        stab[a * slots : (a + 1) * slots, :] = sin_s * cos_a - cos_s * sin_a

    half = n // 2
    ordered = iota((half, n), 0)
    wanted = (
        lax.rem(ordered, eighth) * 4
        + lax.rem(ordered // eighth, 2) * 2
        + ordered // quarter
    )
    pick = one_hot(wanted == iota((half, n), 1))
    lattice = off_ref[...].astype(jnp.float32).astype(jnp.bfloat16)
    off_cols = lax.dot_general(pick, lattice, ACROSS, preferred_element_type=jnp.float32)
    spread = one_hot(iota((kslot, slots), 0) == iota((kslot, slots), 1))
    k_rows = jnp.dot(coords, spread, preferred_element_type=jnp.float32)
    turns = jnp.zeros((half, slots), jnp.float32)
    for x in range(3):
        turns = turns + off_cols[:, x : x + 1] * k_rows[x : x + 1, :]
    cos_t, sin_t = wave(turns)
    count = jnp.full((1, slots), count_ref[0], jnp.int32)
    weight = (1.0 / count.astype(jnp.float32)).astype(jnp.bfloat16).astype(jnp.float32)
    weight = jnp.where(iota((1, slots), 1) < count, weight, 0.0)
    table = jnp.concatenate([cos_t * weight, sin_t * weight], 0).astype(jnp.bfloat16)
    deep = 8 * slots
    rows_of = one_hot(iota((8 * n, n), 0) // 8 == iota((8 * n, n), 1))
    tall = jnp.dot(rows_of, table, preferred_element_type=jnp.float32).astype(jnp.bfloat16)
    lanes_of = one_hot(iota((slots, deep), 0) == lax.rem(iota((slots, deep), 1), slots))
    full = jnp.dot(tall, lanes_of, preferred_element_type=jnp.float32)
    own = lax.rem(iota((8 * n, deep), 0), 8) == iota((8 * n, deep), 1) // slots
    wbd[...] = jnp.where(own, full, 0.0).astype(jnp.bfloat16)

    pl.semaphore_wait(barrier, quarter + 1)

    def compute(c):
        spin, start = c // blocks, lax.rem(c, blocks) * ROWS
        f_re, f_im = fre[spin], fim[spin]
        for j in range(ROWS):
            v = vf[spin, pl.ds(start + j, 1), :]
            v_re, v_im = v[:, :norb], v[:, norb:]
            band = slice(j * slots, (j + 1) * slots)
            scaled[band, :norb] = (v_re * f_re - v_im * f_im).astype(jnp.bfloat16)
            scaled[band, norb:] = (v_re * f_im + v_im * f_re).astype(jnp.bfloat16)
        bare = lax.dot_general(
            scaled[...], right[spin], ACROSS, preferred_element_type=jnp.float32
        )
        here = pl.ds(pl.multiple_of(start * slots, ROWS * slots), ROWS * slots)
        green = bare * ctab[here, :] + pltpu.roll(bare, mag, 1) * stab[here, :]
        green = green.astype(jnp.bfloat16)
        sense = jnp.where(spin == 0, 1.0, -1.0) * -sign
        for part in range(ROWS // 8):
            mixed = jnp.dot(
                wbd[...], green[part * deep : (part + 1) * deep], preferred_element_type=jnp.float32
            )
            even = mixed[: 4 * n].reshape(2, 2, eighth, 8, wide)
            odd = (pltpu.roll(mixed[4 * n :], mag, 1) * sense).reshape(2, 2, eighth, 8, wide)
            rows = slice(part * 8, part * 8 + 8)
            acc[c, :, :, :eighth, rows, :] = even + odd
            acc[c, :, :, eighth:, rows, :] = even - odd

    def copy1(c):
        return pltpu.make_async_remote_copy(
            src_ref=send1.at[c],
            dst_ref=recv1.at[c],
            send_sem=ssem1.at[c],
            recv_sem=rsem1.at[c],
            device_id=mate0,
            device_id_type=pl.DeviceIdType.MESH,
        )

    def copy2(c):
        return pltpu.make_async_remote_copy(
            src_ref=send2.at[c],
            dst_ref=recv2.at[c],
            send_sem=ssem2.at[c],
            recv_sem=rsem2.at[c],
            device_id=mate1,
            device_id_type=pl.DeviceIdType.MESH,
        )

    def copy3(c, k):
        return pltpu.make_async_remote_copy(
            src_ref=send3.at[c, peer(k)],
            dst_ref=recv3.at[c, k - 1],
            send_sem=ssem3.at[c, k - 1],
            recv_sem=rsem3.at[c, k - 1],
            device_id=peer_id(k),
            device_id_type=pl.DeviceIdType.MESH,
        )

    def stage1(c):
        send1[c] = acc[c, 1 - b0].astype(jnp.bfloat16)
        copy1(c).start()

    def stage2(c):
        copy1(c).wait()
        passed = acc[c, b0, 1 - b1] + recv1[c, 1 - b1].astype(jnp.float32)
        send2[c] = passed.astype(jnp.bfloat16)
        copy2(c).start()
        acc2[c] = acc[c, b0, b1] + recv1[c, b1].astype(jnp.float32)

    def stage3(c):
        copy2(c).wait()
        total = acc2[c] + recv2[c].astype(jnp.float32)
        send3[c] = total.astype(jnp.bfloat16)
        for k in range(1, quarter):
            copy3(c, k).start()
        acc2[c] = total
        acc3[c] = acc2[c, q]

    def step(c, carry):
        compute(c)
        stage1(c)

        @pl.when(c >= 1)
        def _():
            stage2(c - 1)

        @pl.when(c >= 2)
        def _():
            stage3(c - 2)

        return carry

    lax.fori_loop(0, chunks, step, 0)
    stage2(chunks - 1)
    stage3(chunks - 2)
    stage3(chunks - 1)

    same = id_col == id_row[:, :mag]
    split = split_ref[...]
    splitting = jnp.where(same, 0.5 * (split + split.T), 0.0)
    member_rows = jnp.where(iota((atoms, mag), 0) == id_row[:, :mag], 1.0, 0.0)
    member_cols = jnp.where(id_col == iota((mag, atoms), 1), 1.0, 0.0)

    def landed(c, carry):
        for k in range(1, quarter):
            copy3(c, k).wait()
        total = acc3[c]
        for k in range(1, quarter):
            total = total + recv3[c, k - 1].astype(jnp.float32)
        acc3[c] = total
        return carry

    lax.fori_loop(0, chunks, landed, 0)
    up = acc3[:blocks].reshape(mag, wide)
    down = acc3[blocks:].reshape(mag, wide)
    left = jnp.dot(splitting, up, precision=HIGH, preferred_element_type=jnp.float32)
    turned = jnp.dot(down.T, splitting, precision=HIGH, preferred_element_type=jnp.float32)
    im_part = left[:, :mag] * turned[mag:] + left[:, mag:] * turned[:mag]
    by_atom = jnp.dot(member_rows, im_part, precision=HIGH, preferred_element_type=jnp.float32)
    pairs = jnp.dot(by_atom, member_cols, precision=HIGH, preferred_element_type=jnp.float32)
    out_ref[0] = -inv_four_pi * pairs


def local(n, *args):
    eigvecs, eigvals, offsets, atom_orbitals = args[0], args[1], args[6], args[7]
    mag, norb = eigvecs.shape[2], eigvals.shape[2]
    slots = -(-eigvals.shape[0] // 16) * 16
    atoms = atom_orbitals.shape[0]
    chunks = 2 * mag // ROWS
    quarter = n // 4
    wide = 2 * mag
    assert offsets.shape[1] == n and n % 8 == 0 and mag % ROWS == 0
    vmem = pl.BlockSpec(memory_space=pltpu.VMEM)
    smem = pl.BlockSpec(memory_space=pltpu.SMEM)
    f32, bf16 = jnp.float32, jnp.bfloat16
    tile = (ROWS, wide)
    dma = pltpu.SemaphoreType.DMA
    return pl.pallas_call(
        functools.partial(kernel, n),
        out_shape=jax.ShapeDtypeStruct((1, atoms, atoms), f32),
        in_specs=[vmem, vmem, vmem, smem, smem, smem, vmem, smem, smem, vmem],
        out_specs=vmem,
        scratch_shapes=[
            pltpu.VMEM((2, mag, 2 * norb), f32),
            pltpu.VMEM((2, wide, 2 * norb), bf16),
            pltpu.VMEM((2, slots, norb), f32),
            pltpu.VMEM((2, slots, norb), f32),
            pltpu.VMEM((2, slots, norb), f32),
            pltpu.VMEM((mag * slots, wide), f32),
            pltpu.VMEM((mag * slots, wide), f32),
            pltpu.VMEM((8 * n, 8 * slots), bf16),
            pltpu.VMEM((ROWS * slots, 2 * norb), bf16),
            pltpu.VMEM((chunks, 2, 2, quarter) + tile, f32),
            pltpu.VMEM((chunks, quarter) + tile, f32),
            pltpu.VMEM((chunks,) + tile, f32),
            pltpu.VMEM((chunks, 2, quarter) + tile, bf16),
            pltpu.VMEM((chunks, 2, quarter) + tile, bf16),
            pltpu.VMEM((chunks, quarter) + tile, bf16),
            pltpu.VMEM((chunks, quarter) + tile, bf16),
            pltpu.VMEM((chunks, quarter) + tile, bf16),
            pltpu.VMEM((chunks, quarter - 1) + tile, bf16),
            dma((chunks,)),
            dma((chunks,)),
            dma((chunks,)),
            dma((chunks,)),
            dma((chunks, quarter - 1)),
            dma((chunks, quarter - 1)),
        ],
        compiler_params=pltpu.CompilerParams(
            collective_id=0, has_side_effects=True, vmem_limit_bytes=48 * 1024 * 1024
        ),
    )(*args)


def solution(mesh):
    placed = (
        P("ka", None, None, None),
        P("ka", None, None),
        P(None, "ka"),
        P("ka"),
        P("grp"),
        P("grp"),
        P(),
        P(),
        P(),
        P(),
    )
    return jax.shard_map(
        functools.partial(local, mesh.shape["ka"]),
        mesh=mesh,
        in_specs=placed,
        out_specs=P(("grp", "ka"), None, None),
        check_vma=False,
    )
```

```python
import functools

import jax
import jax.numpy as jnp
from jax import lax
from jax.experimental import pallas as pl
from jax.experimental.pallas import tpu as pltpu
from jax.sharding import PartitionSpec as P

inv_four_pi = 0.25 / 3.141592653589793
two_pi = 2.0 * 3.141592653589793

ROWS = 16
HIGH = lax.Precision.HIGHEST
ACROSS = (((1,), (1,)), ((), ()))


def wave(turns):
    part = (turns - jnp.round(turns)) * two_pi
    return jnp.cos(part), jnp.sin(part)


def one_hot(condition):
    return jnp.where(condition, 1.0, 0.0).astype(jnp.bfloat16)


def iota(shape, axis):
    return lax.broadcasted_iota(jnp.int32, shape, axis)


def kernel(
    n,
    groups,
    vec_hbm,
    lev_hbm,
    k_hbm,
    count_hbm,
    er_hbm,
    ei_hbm,
    off_hbm,
    orb_hbm,
    pos_hbm,
    split_hbm,
    out_ref,
    vec_ref,
    lev_ref,
    k_ref,
    count_ref,
    er_ref,
    ei_ref,
    off_ref,
    orb_ref,
    pos_ref,
    split_ref,
    vf,
    right,
    flipped,
    levels,
    fre,
    fim,
    ctab,
    stab,
    wbd,
    scaled,
    acc,
    acc2,
    acc3,
    send1,
    recv1,
    send2,
    recv2,
    send3,
    recv3,
    isem,
    ssem1,
    rsem1,
    ssem2,
    rsem2,
    ssem3,
    rsem3,
):
    fetches = [
        pltpu.make_async_copy(source, target, isem.at[i])
        for i, (source, target) in enumerate(
            [
                (vec_hbm, vec_ref),
                (lev_hbm, lev_ref),
                (er_hbm, er_ref),
                (ei_hbm, ei_ref),
                (k_hbm, k_ref),
                (orb_hbm, orb_ref),
                (pos_hbm, pos_ref),
                (off_hbm, off_ref),
                (count_hbm, count_ref),
                (split_hbm, split_ref),
            ]
        )
    ]
    for fetch in fetches:
        fetch.start()

    mag, norb = vec_ref.shape[2], vec_ref.shape[3] // 2
    kslot = lev_ref.shape[0]
    slots = levels.shape[1]
    atoms = orb_ref.shape[0]
    blocks = mag // ROWS
    quarter, eighth = n // 4, n // 8
    wide = 2 * mag

    me = lax.axis_index("ka")
    b0, b1, q = lax.rem(me, 2), lax.rem(me // 2, 2), me // 4
    mate0 = {"ka": me + 1 - 2 * b0}
    mate1 = {"ka": me + 2 - 4 * b1}

    def peer(k):
        return lax.rem(q + k, quarter)

    def peer_id(k):
        return {"ka": peer(k) * 4 + b1 * 2 + b0}

    barrier = pltpu.get_barrier_semaphore()
    for other in [mate0, mate1] + [peer_id(k) for k in range(1, quarter)]:
        pl.semaphore_signal(
            barrier, inc=1, device_id=other, device_id_type=pl.DeviceIdType.MESH
        )
    for fetch in fetches:
        fetch.wait()

    for s in range(kslot):
        row = lev_ref[s].astype(jnp.float32)
        levels[0, s : s + 1, :] = row[0:1]
        levels[1, s : s + 1, :] = row[1:2]
    er, ei = er_ref[0], ei_ref[0]
    for spin in range(2):
        levels[spin, kslot:, :] = jnp.zeros((slots - kslot, norb), jnp.float32)
        vectors = vec_ref[0, spin]
        vf[spin] = vectors.astype(jnp.float32)
        right[spin, :mag, :] = vectors
        right[spin, mag:, :norb] = -vectors[:, norb:]
        right[spin, mag:, norb:] = vectors[:, :norb]
        flipped[spin] = right[spin].T
        shift = er - levels[spin]
        denom = shift * shift + ei * ei
        inverse = 1.0 / denom
        fre[spin] = shift * inverse
        fim[spin] = -ei * inverse

    def scale(i):
        spin, start = i // blocks, i % blocks * ROWS
        f_re, f_im = fre[spin], fim[spin]
        for j in range(ROWS):
            v = vf[spin, start + j : start + j + 1, :]
            v_re, v_im = v[:, :norb], v[:, norb:]
            band = slice(j * slots, (j + 1) * slots)
            scaled[i % 2, band, :norb] = (v_re * f_re - v_im * f_im).astype(jnp.bfloat16)
            scaled[i % 2, band, norb:] = (v_re * f_im + v_im * f_re).astype(jnp.bfloat16)

    scale(0)

    lane = iota((1, wide), 1)
    lane = jnp.where(lane >= mag, lane - mag, lane)
    down_rows = iota((mag, 1), 0)
    id_row = jnp.zeros((1, wide), jnp.int32)
    id_col = jnp.zeros((mag, 1), jnp.int32)
    end = jnp.int32(0)
    for i in range(atoms):
        end = end + orb_ref[i]
        id_row = id_row + jnp.where(lane >= end, 1, 0)
        id_col = id_col + jnp.where(down_rows >= end, 1, 0)

    coords = k_ref[...]
    eye = one_hot(iota((slots, kslot), 0) == iota((slots, kslot), 1))
    k_cols = lax.dot_general(eye, coords, ACROSS, preferred_element_type=jnp.float32)
    kpos = jnp.zeros((slots, wide), jnp.float32)
    for x in range(3):
        site = jnp.zeros((1, wide), jnp.float32)
        for i in range(atoms):
            site = jnp.where(id_row == i, pos_ref[x, i], site)
        kpos = kpos + k_cols[:, x : x + 1] * site
    cos_c, sin_c = wave(kpos)
    sign = jnp.where(iota((1, wide), 1) < mag, -1.0, 1.0)
    cos_s, sin_s = cos_c * sign, sin_c * sign
    for a in range(mag):
        cos_a, sin_a = cos_c[:, a : a + 1], sin_c[:, a : a + 1]
        ctab[a * slots : (a + 1) * slots, :] = cos_c * cos_a + sin_c * sin_a
        stab[a * slots : (a + 1) * slots, :] = sin_s * cos_a - cos_s * sin_a

    half = n // 2
    ordered = iota((half, n), 0)
    wanted = (
        lax.rem(ordered, eighth) * 4
        + lax.rem(ordered // eighth, 2) * 2
        + ordered // quarter
    )
    pick = one_hot(wanted == iota((half, n), 1))
    lattice = off_ref[...].astype(jnp.float32).astype(jnp.bfloat16)
    off_cols = lax.dot_general(pick, lattice, ACROSS, preferred_element_type=jnp.float32)
    spread = one_hot(iota((kslot, slots), 0) == iota((kslot, slots), 1))
    k_rows = jnp.dot(coords, spread, preferred_element_type=jnp.float32)
    turns = jnp.zeros((half, slots), jnp.float32)
    for x in range(3):
        turns = turns + off_cols[:, x : x + 1] * k_rows[x : x + 1, :]
    cos_t, sin_t = wave(turns)
    count = jnp.full((1, slots), count_ref[0], jnp.int32)
    weight = (1.0 / count.astype(jnp.float32)).astype(jnp.bfloat16).astype(jnp.float32)
    weight = jnp.where(iota((1, slots), 1) < count, weight, 0.0)
    table = jnp.concatenate([cos_t * weight, sin_t * weight], 0).astype(jnp.bfloat16)
    deep = 8 * slots
    rows_of = one_hot(iota((8 * n, n), 0) // 8 == iota((8 * n, n), 1))
    tall = jnp.dot(rows_of, table, preferred_element_type=jnp.float32).astype(jnp.bfloat16)
    lanes_of = one_hot(iota((slots, deep), 0) == lax.rem(iota((slots, deep), 1), slots))
    full = jnp.dot(tall, lanes_of, preferred_element_type=jnp.float32)
    own = lax.rem(iota((8 * n, deep), 0), 8) == iota((8 * n, deep), 1) // slots
    wbd[...] = jnp.where(own, full, 0.0).astype(jnp.bfloat16)

    same = id_col == id_row[:, :mag]
    split = split_ref[...]
    splitting = jnp.where(same, 0.5 * (split + split.T), 0.0)
    member_rows = jnp.where(iota((atoms, mag), 0) == id_row[:, :mag], 1.0, 0.0)
    member_cols = jnp.where(id_col == iota((mag, atoms), 1), 1.0, 0.0)

    def mix(i):
        spin, start = i // blocks, i % blocks * ROWS
        bare = jnp.dot(scaled[i % 2], flipped[spin], preferred_element_type=jnp.float32)
        here = slice(start * slots, (start + ROWS) * slots)
        green = bare * ctab[here, :] + pltpu.roll(bare, mag, 1) * stab[here, :]
        green = green.astype(jnp.bfloat16)
        sense = sign if spin else -sign
        for part in range(ROWS // 8):
            mixed = jnp.dot(
                wbd[...], green[part * deep : (part + 1) * deep], preferred_element_type=jnp.float32
            )
            even = mixed[: 4 * n].reshape(2, 2, eighth, 8, wide)
            odd = (pltpu.roll(mixed[4 * n :], mag, 1) * sense).reshape(2, 2, eighth, 8, wide)
            rows = slice(part * 8, part * 8 + 8)
            acc[i, :, :, :eighth, rows, :] = even + odd
            acc[i, :, :, eighth:, rows, :] = even - odd

    def span(g):
        return pl.ds(groups[g][0], groups[g][1])

    def copy1(g):
        return pltpu.make_async_remote_copy(
            src_ref=send1.at[span(g)],
            dst_ref=recv1.at[span(g)],
            send_sem=ssem1.at[g],
            recv_sem=rsem1.at[g],
            device_id=mate0,
            device_id_type=pl.DeviceIdType.MESH,
        )

    def copy2(g):
        return pltpu.make_async_remote_copy(
            src_ref=send2.at[span(g)],
            dst_ref=recv2.at[span(g)],
            send_sem=ssem2.at[g],
            recv_sem=rsem2.at[g],
            device_id=mate1,
            device_id_type=pl.DeviceIdType.MESH,
        )

    def copy3(g, k):
        return pltpu.make_async_remote_copy(
            src_ref=send3.at[peer(k), span(g)],
            dst_ref=recv3.at[k - 1, span(g)],
            send_sem=ssem3.at[g, k - 1],
            recv_sem=rsem3.at[g, k - 1],
            device_id=peer_id(k),
            device_id_type=pl.DeviceIdType.MESH,
        )

    def members(g):
        return range(groups[g][0], groups[g][0] + groups[g][1])

    def stage1(g):
        if g == 0:
            pl.semaphore_wait(barrier, quarter + 1)
        for i in members(g):
            send1[i] = acc[i, 1 - b0].astype(jnp.bfloat16)
        copy1(g).start()

    def stage2(g):
        copy1(g).wait()
        for i in members(g):
            passed = acc[i, b0, 1 - b1] + recv1[i, 1 - b1].astype(jnp.float32)
            send2[i] = passed.astype(jnp.bfloat16)
        copy2(g).start()
        for i in members(g):
            acc2[i] = acc[i, b0, b1] + recv1[i, b1].astype(jnp.float32)

    def stage3(g):
        copy2(g).wait()
        for i in members(g):
            total = acc2[i] + recv2[i].astype(jnp.float32)
            send3[:, i] = total.astype(jnp.bfloat16)
            acc2[i] = total
        for k in range(1, quarter):
            copy3(g, k).start()
        for i in members(g):
            acc3[i] = acc2[i, q]

    def stage4(g):
        for k in range(1, quarter):
            copy3(g, k).wait()
        for i in members(g):
            total = acc3[i]
            for k in range(1, quarter):
                total = total + recv3[k - 1, i].astype(jnp.float32)
            acc3[i] = total

    due = {}
    for g, (first, length) in enumerate(groups):
        for wait, stage in enumerate([stage1, stage2, stage3, stage4]):
            due.setdefault(first + length - 1 + wait, []).insert(0, (stage, g))
    left = None
    for i in range(2 * blocks + 3):
        if i + 1 < 2 * blocks:
            scale(i + 1)
        if i < 2 * blocks:
            mix(i)
        for stage, g in due.get(i, []):
            stage(g)
        if i == 2 * blocks:
            up = acc3[:blocks].reshape(mag, wide)
            left = jnp.dot(splitting, up, precision=HIGH, preferred_element_type=jnp.float32)

    down = acc3[blocks:].reshape(mag, wide)
    turned = jnp.dot(down.T, splitting, precision=HIGH, preferred_element_type=jnp.float32)
    im_part = left[:, :mag] * turned[mag:] + left[:, mag:] * turned[:mag]
    by_atom = jnp.dot(member_rows, im_part, precision=HIGH, preferred_element_type=jnp.float32)
    pairs = jnp.dot(by_atom, member_cols, precision=HIGH, preferred_element_type=jnp.float32)
    out_ref[0] = -inv_four_pi * pairs


def local(n, *args):
    eigvecs, eigvals, offsets, atom_orbitals = args[0], args[1], args[6], args[7]
    mag, norb = eigvecs.shape[2], eigvals.shape[2]
    slots = -(-eigvals.shape[0] // 16) * 16
    atoms = atom_orbitals.shape[0]
    chunks = 2 * mag // ROWS
    quarter = n // 4
    wide = 2 * mag
    assert offsets.shape[1] == n and n % 8 == 0 and mag % ROWS == 0
    groups, first = [], 0
    while first < chunks:
        length = 2 if chunks - first > 3 else 1
        groups.append((first, length))
        first += length
    sends = len(groups)
    f32, bf16 = jnp.float32, jnp.bfloat16
    tile = (ROWS, wide)
    dma = pltpu.SemaphoreType.DMA
    on_smem = (3, 4, 5, 7, 8)
    staged = [
        (pltpu.SMEM if i in on_smem else pltpu.VMEM)(arg.shape, arg.dtype)
        for i, arg in enumerate(args)
    ]
    return pl.pallas_call(
        functools.partial(kernel, n, groups),
        out_shape=jax.ShapeDtypeStruct((1, atoms, atoms), f32),
        in_specs=[pl.BlockSpec(memory_space=pltpu.HBM)] * len(args),
        out_specs=pl.BlockSpec(memory_space=pltpu.VMEM),
        scratch_shapes=staged
        + [
            pltpu.VMEM((2, mag, 2 * norb), f32),
            pltpu.VMEM((2, wide, 2 * norb), bf16),
            pltpu.VMEM((2, 2 * norb, wide), bf16),
            pltpu.VMEM((2, slots, norb), f32),
            pltpu.VMEM((2, slots, norb), f32),
            pltpu.VMEM((2, slots, norb), f32),
            pltpu.VMEM((mag * slots, wide), f32),
            pltpu.VMEM((mag * slots, wide), f32),
            pltpu.VMEM((8 * n, 8 * slots), bf16),
            pltpu.VMEM((2, ROWS * slots, 2 * norb), bf16),
            pltpu.VMEM((chunks, 2, 2, quarter) + tile, f32),
            pltpu.VMEM((chunks, quarter) + tile, f32),
            pltpu.VMEM((chunks,) + tile, f32),
            pltpu.VMEM((chunks, 2, quarter) + tile, bf16),
            pltpu.VMEM((chunks, 2, quarter) + tile, bf16),
            pltpu.VMEM((chunks, quarter) + tile, bf16),
            pltpu.VMEM((chunks, quarter) + tile, bf16),
            pltpu.VMEM((quarter, chunks) + tile, bf16),
            pltpu.VMEM((quarter - 1, chunks) + tile, bf16),
            dma((len(args),)),
            dma((sends,)),
            dma((sends,)),
            dma((sends,)),
            dma((sends,)),
            dma((sends, quarter - 1)),
            dma((sends, quarter - 1)),
        ],
        compiler_params=pltpu.CompilerParams(
            collective_id=0, has_side_effects=True, vmem_limit_bytes=48 * 1024 * 1024
        ),
    )(*args)


def solution(mesh):
    placed = (
        P("ka", None, None, None),
        P("ka", None, None),
        P(None, "ka"),
        P("ka"),
        P("grp"),
        P("grp"),
        P(),
        P(),
        P(),
        P(),
    )
    return jax.shard_map(
        functools.partial(local, mesh.shape["ka"]),
        mesh=mesh,
        in_specs=placed,
        out_specs=P(("grp", "ka"), None, None),
        check_vma=False,
    )
```

```python
import functools

import jax
import jax.numpy as jnp
from jax import lax
from jax.experimental import pallas as pl
from jax.experimental.pallas import tpu as pltpu
from jax.sharding import PartitionSpec as P

inv_four_pi = 0.25 / 3.141592653589793
two_pi = 2.0 * 3.141592653589793

ROWS = 16
HIGH = lax.Precision.HIGHEST
ACROSS = (((1,), (1,)), ((), ()))


def wave(turns):
    part = (turns - jnp.round(turns)) * two_pi
    return jnp.cos(part), jnp.sin(part)


def one_hot(condition):
    return jnp.where(condition, 1.0, 0.0).astype(jnp.bfloat16)


def iota(shape, axis):
    return lax.broadcasted_iota(jnp.int32, shape, axis)


def kernel(
    n,
    vec_hbm,
    lev_hbm,
    k_hbm,
    count_hbm,
    er_hbm,
    ei_hbm,
    off_hbm,
    orb_hbm,
    pos_hbm,
    split_hbm,
    out_ref,
    vec_ref,
    lev_ref,
    k_ref,
    count_ref,
    er_ref,
    ei_ref,
    off_ref,
    orb_ref,
    pos_ref,
    split_ref,
    vf,
    right,
    flipped,
    levels,
    fre,
    fim,
    ctab,
    stab,
    wbd,
    scaled_a,
    scaled_b,
    acc,
    acc2,
    acc3,
    recv1,
    send2,
    recv2,
    recv3,
    isem,
    ssem1,
    rsem1,
    ssem2,
    rsem2,
    ssem3,
    rsem3,
):
    fetches = [
        pltpu.make_async_copy(source, target, isem.at[i])
        for i, (source, target) in enumerate(
            [
                (vec_hbm, vec_ref),
                (lev_hbm, lev_ref),
                (er_hbm, er_ref),
                (ei_hbm, ei_ref),
                (k_hbm, k_ref),
                (orb_hbm, orb_ref),
                (pos_hbm, pos_ref),
                (off_hbm, off_ref),
                (count_hbm, count_ref),
                (split_hbm, split_ref),
            ]
        )
    ]
    for fetch in fetches:
        fetch.start()

    mag, norb = vec_ref.shape[2], vec_ref.shape[3] // 2
    kslot = lev_ref.shape[0]
    slots = levels.shape[1]
    atoms = orb_ref.shape[0]
    blocks = mag // ROWS
    quarter, eighth = n // 4, n // 8
    wide = 2 * mag

    me = lax.axis_index("ka")
    b0, b1, q = lax.rem(me, 2), lax.rem(me // 2, 2), me // 4
    mate0 = {"ka": me + 1 - 2 * b0}
    mate1 = {"ka": me + 2 - 4 * b1}

    def peer(k):
        return lax.rem(q + k, quarter)

    def peer_id(k):
        return {"ka": peer(k) * 4 + b1 * 2 + b0}

    barrier = pltpu.get_barrier_semaphore()
    for other in [mate0, mate1] + [peer_id(k) for k in range(1, quarter)]:
        pl.semaphore_signal(
            barrier, inc=1, device_id=other, device_id_type=pl.DeviceIdType.MESH
        )
    for fetch in fetches:
        fetch.wait()

    for s in range(kslot):
        row = lev_ref[s].astype(jnp.float32)
        levels[0, s : s + 1, :] = row[0:1]
        levels[1, s : s + 1, :] = row[1:2]
    er, ei = er_ref[0], ei_ref[0]

    def prepare(spin, carry):
        levels[spin, kslot:, :] = jnp.zeros((slots - kslot, norb), jnp.float32)
        vectors = vec_ref[0, spin]
        vf[spin] = vectors.astype(jnp.float32)
        right[spin, :mag, :] = vectors
        right[spin, mag:, :norb] = -vectors[:, norb:]
        right[spin, mag:, norb:] = vectors[:, :norb]
        flipped[spin] = right[spin].T
        shift = er - levels[spin]
        denom = shift * shift + ei * ei
        inverse = 1.0 / denom
        fre[spin] = shift * inverse
        fim[spin] = -ei * inverse
        return carry

    lax.fori_loop(0, 2, prepare, 0)

    def scale(h, scaled):
        spin, start = h // (2 * blocks), lax.rem(h, 2 * blocks) * 8
        f_re, f_im = fre[spin], fim[spin]
        for j in range(8):
            v = vf[spin, pl.ds(start + j, 1), :]
            v_re, v_im = v[:, :norb], v[:, norb:]
            band = slice(j * slots, (j + 1) * slots)
            scaled[band, :norb] = (v_re * f_re - v_im * f_im).astype(jnp.bfloat16)
            scaled[band, norb:] = (v_re * f_im + v_im * f_re).astype(jnp.bfloat16)

    scale(0, scaled_a)

    lane = iota((1, wide), 1)
    lane = jnp.where(lane >= mag, lane - mag, lane)
    down_rows = iota((mag, 1), 0)
    id_row = jnp.zeros((1, wide), jnp.int32)
    id_col = jnp.zeros((mag, 1), jnp.int32)
    end = jnp.int32(0)
    for i in range(atoms):
        end = end + orb_ref[i]
        id_row = id_row + jnp.where(lane >= end, 1, 0)
        id_col = id_col + jnp.where(down_rows >= end, 1, 0)

    coords = k_ref[...]
    eye = one_hot(iota((slots, kslot), 0) == iota((slots, kslot), 1))
    k_cols = lax.dot_general(eye, coords, ACROSS, preferred_element_type=jnp.float32)
    kpos = jnp.zeros((slots, wide), jnp.float32)
    for x in range(3):
        site = jnp.zeros((1, wide), jnp.float32)
        for i in range(atoms):
            site = jnp.where(id_row == i, pos_ref[x, i], site)
        kpos = kpos + k_cols[:, x : x + 1] * site
    cos_c, sin_c = wave(kpos)
    sign = jnp.where(iota((1, wide), 1) < mag, -1.0, 1.0)
    cos_s, sin_s = cos_c * sign, sin_c * sign
    deep = 8 * slots

    def gauge(h, carry):
        cos_r = pltpu.roll(cos_c, wide - 8 * h, 1)
        sin_r = pltpu.roll(sin_c, wide - 8 * h, 1)
        for j in range(8):
            cos_a, sin_a = cos_r[:, j : j + 1], sin_r[:, j : j + 1]
            here = pl.ds(pl.multiple_of(h * deep + j * slots, slots), slots)
            ctab[here, :] = cos_c * cos_a + sin_c * sin_a
            stab[here, :] = sin_s * cos_a - cos_s * sin_a
        return carry

    lax.fori_loop(0, mag // 8, gauge, 0)

    half = n // 2
    ordered = iota((half, n), 0)
    wanted = (
        lax.rem(ordered, eighth) * 4
        + lax.rem(ordered // eighth, 2) * 2
        + ordered // quarter
    )
    pick = one_hot(wanted == iota((half, n), 1))
    lattice = off_ref[...].astype(jnp.float32).astype(jnp.bfloat16)
    off_cols = lax.dot_general(pick, lattice, ACROSS, preferred_element_type=jnp.float32)
    spread = one_hot(iota((kslot, slots), 0) == iota((kslot, slots), 1))
    k_rows = jnp.dot(coords, spread, preferred_element_type=jnp.float32)
    turns = jnp.zeros((half, slots), jnp.float32)
    for x in range(3):
        turns = turns + off_cols[:, x : x + 1] * k_rows[x : x + 1, :]
    cos_t, sin_t = wave(turns)
    count = jnp.full((1, slots), count_ref[0], jnp.int32)
    weight = (1.0 / count.astype(jnp.float32)).astype(jnp.bfloat16).astype(jnp.float32)
    weight = jnp.where(iota((1, slots), 1) < count, weight, 0.0)
    table = jnp.concatenate([cos_t * weight, sin_t * weight], 0).astype(jnp.bfloat16)
    rows_of = one_hot(iota((8 * n, n), 0) // 8 == iota((8 * n, n), 1))
    tall = jnp.dot(rows_of, table, preferred_element_type=jnp.float32).astype(jnp.bfloat16)
    lanes_of = one_hot(iota((slots, deep), 0) == lax.rem(iota((slots, deep), 1), slots))
    full = jnp.dot(tall, lanes_of, preferred_element_type=jnp.float32)
    own = lax.rem(iota((8 * n, deep), 0), 8) == iota((8 * n, deep), 1) // slots
    wbd[...] = jnp.where(own, full, 0.0).astype(jnp.bfloat16)

    same = id_col == id_row[:, :mag]
    split = split_ref[...]
    splitting = jnp.where(same, 0.5 * (split + split.T), 0.0)
    member_rows = jnp.where(iota((atoms, mag), 0) == id_row[:, :mag], 1.0, 0.0)
    member_cols = jnp.where(id_col == iota((mag, atoms), 1), 1.0, 0.0)

    def mix(h, part, scaled):
        spin, start = h // (2 * blocks), lax.rem(h, 2 * blocks) * deep
        bare = jnp.dot(scaled[...], flipped[spin], preferred_element_type=jnp.float32)
        here = pl.ds(pl.multiple_of(start, deep), deep)
        green = bare * ctab[here, :] + pltpu.roll(bare, mag, 1) * stab[here, :]
        mixed = jnp.dot(
            wbd[...], green.astype(jnp.bfloat16), preferred_element_type=jnp.float32
        )
        sense = jnp.where(spin == 0, 1.0, -1.0) * -sign
        even = mixed[: 4 * n].reshape(2, 2, eighth, 8, wide)
        odd = (pltpu.roll(mixed[4 * n :], mag, 1) * sense).reshape(2, 2, eighth, 8, wide)
        rows = slice(part * 8, part * 8 + 8)
        c = h // 2
        acc[c, :, :, :eighth, rows, :] = even + odd
        acc[c, :, :, eighth:, rows, :] = even - odd

    def copy1(c):
        return pltpu.make_async_remote_copy(
            src_ref=acc.at[c, 1 - b0],
            dst_ref=recv1.at[c],
            send_sem=ssem1.at[c],
            recv_sem=rsem1.at[c],
            device_id=mate0,
            device_id_type=pl.DeviceIdType.MESH,
        )

    def copy2(c):
        return pltpu.make_async_remote_copy(
            src_ref=send2.at[c],
            dst_ref=recv2.at[c],
            send_sem=ssem2.at[c],
            recv_sem=rsem2.at[c],
            device_id=mate1,
            device_id_type=pl.DeviceIdType.MESH,
        )

    def copy3(c, k):
        return pltpu.make_async_remote_copy(
            src_ref=acc2.at[c, peer(k)],
            dst_ref=recv3.at[c, k - 1],
            send_sem=ssem3.at[c, k - 1],
            recv_sem=rsem3.at[c, k - 1],
            device_id=peer_id(k),
            device_id_type=pl.DeviceIdType.MESH,
        )

    def stage1(c):
        copy1(c).start()

    def stage2(c):
        copy1(c).wait()
        send2[c] = acc[c, b0, 1 - b1] + recv1[c, 1 - b1]
        copy2(c).start()
        acc2[c] = acc[c, b0, b1] + recv1[c, b1]

    def stage3(c):
        copy2(c).wait()
        acc2[c] = acc2[c] + recv2[c]
        for k in range(1, quarter):
            copy3(c, k).start()
        acc3[c] = acc2[c, q]

    def stage4(c, carry):
        for k in range(1, quarter):
            copy3(c, k).wait()
        total = acc3[c]
        for k in range(1, quarter):
            total = total + recv3[c, k - 1]
        acc3[c] = total
        return carry

    chunks = 2 * blocks
    pl.semaphore_wait(barrier, quarter + 1)

    def step(c, carry):
        scale(2 * c + 1, scaled_b)
        mix(2 * c, 0, scaled_a)
        scale(jnp.minimum(2 * c + 2, 2 * chunks - 1), scaled_a)
        mix(2 * c + 1, 1, scaled_b)
        stage1(c)

        @pl.when(c >= 1)
        def _():
            stage2(c - 1)

        @pl.when(c >= 2)
        def _():
            stage3(c - 2)

        return carry

    lax.fori_loop(0, chunks, step, 0)
    stage2(chunks - 1)
    stage3(chunks - 2)
    lax.fori_loop(0, blocks, stage4, 0)
    up = acc3[:blocks].reshape(mag, wide)
    left = jnp.dot(splitting, up, precision=HIGH, preferred_element_type=jnp.float32)
    stage3(chunks - 1)
    lax.fori_loop(blocks, chunks, stage4, 0)

    down = acc3[blocks:].reshape(mag, wide)
    turned = jnp.dot(down.T, splitting, precision=HIGH, preferred_element_type=jnp.float32)
    im_part = left[:, :mag] * turned[mag:] + left[:, mag:] * turned[:mag]
    by_atom = jnp.dot(member_rows, im_part, precision=HIGH, preferred_element_type=jnp.float32)
    pairs = jnp.dot(by_atom, member_cols, precision=HIGH, preferred_element_type=jnp.float32)
    out_ref[0] = -inv_four_pi * pairs


def local(n, *args):
    eigvecs, eigvals, offsets, atom_orbitals = args[0], args[1], args[6], args[7]
    mag, norb = eigvecs.shape[2], eigvals.shape[2]
    slots = -(-eigvals.shape[0] // 16) * 16
    atoms = atom_orbitals.shape[0]
    chunks = 2 * mag // ROWS
    quarter = n // 4
    wide = 2 * mag
    assert offsets.shape[1] == n and n % 8 == 0 and mag % ROWS == 0
    sends = chunks
    f32, bf16 = jnp.float32, jnp.bfloat16
    tile = (ROWS, wide)
    dma = pltpu.SemaphoreType.DMA
    on_smem = (3, 4, 5, 7, 8)
    staged = [
        (pltpu.SMEM if i in on_smem else pltpu.VMEM)(arg.shape, arg.dtype)
        for i, arg in enumerate(args)
    ]
    return pl.pallas_call(
        functools.partial(kernel, n),
        out_shape=jax.ShapeDtypeStruct((1, atoms, atoms), f32),
        in_specs=[pl.BlockSpec(memory_space=pltpu.HBM)] * len(args),
        out_specs=pl.BlockSpec(memory_space=pltpu.VMEM),
        scratch_shapes=staged
        + [
            pltpu.VMEM((2, mag, 2 * norb), f32),
            pltpu.VMEM((2, wide, 2 * norb), bf16),
            pltpu.VMEM((2, 2 * norb, wide), bf16),
            pltpu.VMEM((2, slots, norb), f32),
            pltpu.VMEM((2, slots, norb), f32),
            pltpu.VMEM((2, slots, norb), f32),
            pltpu.VMEM((mag * slots, wide), f32),
            pltpu.VMEM((mag * slots, wide), f32),
            pltpu.VMEM((8 * n, 8 * slots), bf16),
            pltpu.VMEM((8 * slots, 2 * norb), bf16),
            pltpu.VMEM((8 * slots, 2 * norb), bf16),
            pltpu.VMEM((chunks, 2, 2, quarter) + tile, f32),
            pltpu.VMEM((chunks, quarter) + tile, f32),
            pltpu.VMEM((chunks,) + tile, f32),
            pltpu.VMEM((chunks, 2, quarter) + tile, f32),
            pltpu.VMEM((chunks, quarter) + tile, f32),
            pltpu.VMEM((chunks, quarter) + tile, f32),
            pltpu.VMEM((chunks, quarter - 1) + tile, f32),
            dma((len(args),)),
            dma((sends,)),
            dma((sends,)),
            dma((sends,)),
            dma((sends,)),
            dma((sends, quarter - 1)),
            dma((sends, quarter - 1)),
        ],
        compiler_params=pltpu.CompilerParams(
            collective_id=0, has_side_effects=True, vmem_limit_bytes=63 * 1024 * 1024
        ),
    )(*args)


def solution(mesh):
    placed = (
        P("ka", None, None, None),
        P("ka", None, None),
        P(None, "ka"),
        P("ka"),
        P("grp"),
        P("grp"),
        P(),
        P(),
        P(),
        P(),
    )
    return jax.shard_map(
        functools.partial(local, mesh.shape["ka"]),
        mesh=mesh,
        in_specs=placed,
        out_specs=P(("grp", "ka"), None, None),
        check_vma=False,
    )
```

```python
import functools

import jax
import jax.numpy as jnp
from jax import lax
from jax.experimental import pallas as pl
from jax.experimental.pallas import tpu as pltpu
from jax.sharding import PartitionSpec as P

inv_four_pi = 0.25 / 3.141592653589793
two_pi = 2.0 * 3.141592653589793

ROWS = 16
HIGH = lax.Precision.HIGHEST
PIECE = 128
ACROSS = (((1,), (1,)), ((), ()))


def wave(turns):
    def cosine(part):
        part = part - jnp.round(part)
        x = (0.25 - jnp.abs(part)) * two_pi
        u = x * x
        series = 1.0 / 6227020800.0
        for term in (-1.0 / 39916800.0, 1.0 / 362880.0, -1.0 / 5040.0, 1.0 / 120.0, -1.0 / 6.0):
            series = series * u + term
        return x + x * (u * series)

    turns = turns - jnp.round(turns)
    return cosine(turns), cosine(turns - 0.25)


def one_hot(condition):
    return jnp.where(condition, 1.0, 0.0).astype(jnp.bfloat16)


def iota(shape, axis):
    return lax.broadcasted_iota(jnp.int32, shape, axis)


def kernel(
    n,
    vec_hbm,
    lev_hbm,
    k_hbm,
    count_hbm,
    er_hbm,
    ei_hbm,
    off_hbm,
    orb_hbm,
    pos_hbm,
    split_hbm,
    out_ref,
    vec_ref,
    lev_ref,
    k_ref,
    count_ref,
    er_ref,
    ei_ref,
    off_ref,
    orb_ref,
    pos_ref,
    split_ref,
    vf,
    right,
    flipped,
    levels,
    fre,
    fim,
    ctab,
    stab,
    wbd,
    scaled,
    acc,
    acc2,
    acc3,
    recv1,
    send2,
    recv2,
    recv3,
    isem,
    ssem1,
    rsem1,
    ssem2,
    rsem2,
    ssem3,
    rsem3,
):
    fetches = [
        pltpu.make_async_copy(source, target, isem.at[i])
        for i, (source, target) in enumerate(
            [
                (vec_hbm, vec_ref),
                (lev_hbm, lev_ref),
                (er_hbm, er_ref),
                (ei_hbm, ei_ref),
                (k_hbm, k_ref),
                (orb_hbm, orb_ref),
                (pos_hbm, pos_ref),
                (off_hbm, off_ref),
                (count_hbm, count_ref),
                (split_hbm, split_ref),
            ]
        )
    ]
    for fetch in fetches:
        fetch.start()

    mag, norb = vec_ref.shape[2], vec_ref.shape[3] // 2
    kslot = lev_ref.shape[0]
    slots = levels.shape[1]
    atoms = orb_ref.shape[0]
    blocks = mag // ROWS
    pieces = norb // PIECE
    quarter, eighth = n // 4, n // 8
    wide = 2 * mag

    me = lax.axis_index("ka")
    b0, b1, q = lax.rem(me, 2), lax.rem(me // 2, 2), me // 4
    mate0 = {"ka": me + 1 - 2 * b0}
    mate1 = {"ka": me + 2 - 4 * b1}

    def peer(k):
        return lax.rem(q + k, quarter)

    def peer_id(k):
        return {"ka": peer(k) * 4 + b1 * 2 + b0}

    barrier = pltpu.get_barrier_semaphore()
    for other in [mate0, mate1] + [peer_id(k) for k in range(1, quarter)]:
        pl.semaphore_signal(
            barrier, inc=1, device_id=other, device_id_type=pl.DeviceIdType.MESH
        )
    for fetch in fetches:
        fetch.wait()

    for s in range(kslot):
        row = lev_ref[s].astype(jnp.float32)
        levels[0, s : s + 1, :] = row[0:1]
        levels[1, s : s + 1, :] = row[1:2]
    er, ei = er_ref[0], ei_ref[0]

    def prepare(spin, carry):
        levels[spin, kslot:, :] = jnp.zeros((slots - kslot, norb), jnp.float32)
        vectors = vec_ref[0, spin]
        vf[spin] = vectors.astype(jnp.float32)
        for t in range(pieces):
            re_part = vectors[:, t * PIECE : (t + 1) * PIECE]
            im_part = vectors[:, norb + t * PIECE : norb + (t + 1) * PIECE]
            right[:mag, :PIECE] = re_part
            right[:mag, PIECE:] = im_part
            right[mag:, :PIECE] = -im_part
            right[mag:, PIECE:] = re_part
            flipped[spin, t] = right[...].T
        shift = er - levels[spin]
        denom = shift * shift + ei * ei
        inverse = 1.0 / denom
        fre[spin] = shift * inverse
        fim[spin] = -ei * inverse
        return carry

    lax.fori_loop(0, 2, prepare, 0)

    lane = iota((1, wide), 1)
    lane = jnp.where(lane >= mag, lane - mag, lane)
    down_rows = iota((mag, 1), 0)
    id_row = jnp.zeros((1, wide), jnp.int32)
    id_col = jnp.zeros((mag, 1), jnp.int32)
    end = jnp.int32(0)
    for i in range(atoms):
        end = end + orb_ref[i]
        id_row = id_row + jnp.where(lane >= end, 1, 0)
        id_col = id_col + jnp.where(down_rows >= end, 1, 0)

    coords = k_ref[...]
    eye = one_hot(iota((slots, kslot), 0) == iota((slots, kslot), 1))
    k_cols = lax.dot_general(eye, coords, ACROSS, preferred_element_type=jnp.float32)
    kpos = jnp.zeros((slots, wide), jnp.float32)
    for x in range(3):
        site = jnp.zeros((1, wide), jnp.float32)
        for i in range(atoms):
            site = jnp.where(id_row == i, pos_ref[x, i], site)
        kpos = kpos + k_cols[:, x : x + 1] * site
    cos_c, sin_c = wave(kpos)
    sign = jnp.where(iota((1, wide), 1) < mag, -1.0, 1.0)
    cos_s, sin_s = cos_c * sign, sin_c * sign
    deep = 8 * slots

    def gauge(h, carry):
        cos_r = pltpu.roll(cos_c, wide - 8 * h, 1)
        sin_r = pltpu.roll(sin_c, wide - 8 * h, 1)
        for j in range(8):
            cos_a, sin_a = cos_r[:, j : j + 1], sin_r[:, j : j + 1]
            here = pl.ds(pl.multiple_of(h * deep + j * slots, slots), slots)
            ctab[here, :] = cos_c * cos_a + sin_c * sin_a
            stab[here, :] = sin_s * cos_a - cos_s * sin_a
        return carry

    lax.fori_loop(0, mag // 8, gauge, 0)

    half = n // 2
    ordered = iota((half, n), 0)
    wanted = (
        lax.rem(ordered, eighth) * 4
        + lax.rem(ordered // eighth, 2) * 2
        + ordered // quarter
    )
    pick = one_hot(wanted == iota((half, n), 1))
    lattice = off_ref[...].astype(jnp.float32).astype(jnp.bfloat16)
    off_cols = lax.dot_general(pick, lattice, ACROSS, preferred_element_type=jnp.float32)
    spread = one_hot(iota((kslot, slots), 0) == iota((kslot, slots), 1))
    k_rows = jnp.dot(coords, spread, preferred_element_type=jnp.float32)
    turns = jnp.zeros((half, slots), jnp.float32)
    for x in range(3):
        turns = turns + off_cols[:, x : x + 1] * k_rows[x : x + 1, :]
    cos_t, sin_t = wave(turns)
    count = jnp.full((1, slots), count_ref[0], jnp.int32)
    weight = (1.0 / count.astype(jnp.float32)).astype(jnp.bfloat16).astype(jnp.float32)
    weight = jnp.where(iota((1, slots), 1) < count, weight, 0.0)
    table = jnp.concatenate([cos_t * weight, sin_t * weight], 0).astype(jnp.bfloat16)
    rows_of = one_hot(iota((8 * n, n), 0) // 8 == iota((8 * n, n), 1))
    tall = jnp.dot(rows_of, table, preferred_element_type=jnp.float32).astype(jnp.bfloat16)
    lanes_of = one_hot(iota((slots, deep), 0) == lax.rem(iota((slots, deep), 1), slots))
    full = jnp.dot(tall, lanes_of, preferred_element_type=jnp.float32)
    own = lax.rem(iota((8 * n, deep), 0), 8) == iota((8 * n, deep), 1) // slots
    wbd[...] = jnp.where(own, full, 0.0).astype(jnp.bfloat16)

    same = id_col == id_row[:, :mag]
    split = split_ref[...]
    splitting = jnp.where(same, 0.5 * (split + split.T), 0.0)
    member_rows = jnp.where(iota((atoms, mag), 0) == id_row[:, :mag], 1.0, 0.0)
    member_cols = jnp.where(id_col == iota((mag, atoms), 1), 1.0, 0.0)

    def compute(c):
        spin, start = c // blocks, lax.rem(c, blocks) * ROWS
        bare = None
        for t in range(pieces):
            at = slice(t * PIECE, (t + 1) * PIECE)
            f_re, f_im = fre[spin, :, at], fim[spin, :, at]
            mirror = slice(norb + t * PIECE, norb + (t + 1) * PIECE)
            these = pl.ds(pl.multiple_of(start, ROWS), ROWS)
            rows_re, rows_im = vf[spin, these, at], vf[spin, these, mirror]
            for j in range(ROWS):
                v_re, v_im = rows_re[j : j + 1], rows_im[j : j + 1]
                band = slice(j * slots, (j + 1) * slots)
                scaled[t, band, :PIECE] = (v_re * f_re - v_im * f_im).astype(jnp.bfloat16)
                scaled[t, band, PIECE:] = (v_re * f_im + v_im * f_re).astype(jnp.bfloat16)
            part = jnp.dot(scaled[t], flipped[spin, t], preferred_element_type=jnp.float32)
            bare = part if t == 0 else bare + part
        here = pl.ds(pl.multiple_of(start * slots, ROWS * slots), ROWS * slots)
        green = bare * ctab[here, :] + pltpu.roll(bare, mag, 1) * stab[here, :]
        green = green.astype(jnp.bfloat16)
        side = jnp.concatenate([green[:deep], green[deep:]], 1)
        mixed = jnp.dot(wbd[...], side, preferred_element_type=jnp.float32)
        sense = jnp.where(spin == 0, 1.0, -1.0) * -sign
        for part in range(ROWS // 8):
            half_mixed = mixed[:, part * wide : (part + 1) * wide]
            even = half_mixed[: 4 * n].reshape(2, 2, eighth, 8, wide)
            odd = pltpu.roll(half_mixed[4 * n :], mag, 1) * sense
            odd = odd.reshape(2, 2, eighth, 8, wide)
            rows = slice(part * 8, part * 8 + 8)
            acc[c, :, :, :eighth, rows, :] = even + odd
            acc[c, :, :, eighth:, rows, :] = even - odd

    def copy1(c):
        return pltpu.make_async_remote_copy(
            src_ref=acc.at[c, 1 - b0],
            dst_ref=recv1.at[c],
            send_sem=ssem1.at[c],
            recv_sem=rsem1.at[c],
            device_id=mate0,
            device_id_type=pl.DeviceIdType.MESH,
        )

    def copy2(c):
        return pltpu.make_async_remote_copy(
            src_ref=send2.at[c],
            dst_ref=recv2.at[c],
            send_sem=ssem2.at[c],
            recv_sem=rsem2.at[c],
            device_id=mate1,
            device_id_type=pl.DeviceIdType.MESH,
        )

    def copy3(c, k):
        return pltpu.make_async_remote_copy(
            src_ref=acc2.at[c, peer(k)],
            dst_ref=recv3.at[c, k - 1],
            send_sem=ssem3.at[c, k - 1],
            recv_sem=rsem3.at[c, k - 1],
            device_id=peer_id(k),
            device_id_type=pl.DeviceIdType.MESH,
        )

    def stage1(c):
        copy1(c).start()

    def stage2(c):
        copy1(c).wait()
        send2[c] = acc[c, b0, 1 - b1] + recv1[c, 1 - b1]
        copy2(c).start()
        acc2[c] = acc[c, b0, b1] + recv1[c, b1]

    def stage3(c):
        copy2(c).wait()
        acc2[c] = acc2[c] + recv2[c]
        for k in range(1, quarter):
            copy3(c, k).start()
        acc3[c] = acc2[c, q]

    def stage4(c, carry):
        for k in range(1, quarter):
            copy3(c, k).wait()
        total = acc3[c]
        for k in range(1, quarter):
            total = total + recv3[c, k - 1]
        acc3[c] = total
        return carry

    chunks = 2 * blocks
    pl.semaphore_wait(barrier, quarter + 1)

    def step(c, carry):
        compute(c)
        stage1(c)

        @pl.when(c >= 1)
        def _():
            stage2(c - 1)

        @pl.when(c >= 2)
        def _():
            stage3(c - 2)

        return carry

    lax.fori_loop(0, chunks, step, 0)
    stage2(chunks - 1)
    stage3(chunks - 2)
    lax.fori_loop(0, blocks, stage4, 0)
    up = acc3[:blocks].reshape(mag, wide)
    left = jnp.dot(splitting, up, precision=HIGH, preferred_element_type=jnp.float32)
    stage3(chunks - 1)
    lax.fori_loop(blocks, chunks, stage4, 0)

    down = acc3[blocks:].reshape(mag, wide)
    turned = jnp.dot(down.T, splitting, precision=HIGH, preferred_element_type=jnp.float32)
    im_part = left[:, :mag] * turned[mag:] + left[:, mag:] * turned[:mag]
    by_atom = jnp.dot(member_rows, im_part, precision=HIGH, preferred_element_type=jnp.float32)
    pairs = jnp.dot(by_atom, member_cols, precision=HIGH, preferred_element_type=jnp.float32)
    out_ref[0] = -inv_four_pi * pairs


def local(n, *args):
    eigvecs, eigvals, offsets, atom_orbitals = args[0], args[1], args[6], args[7]
    mag, norb = eigvecs.shape[2], eigvals.shape[2]
    slots = -(-eigvals.shape[0] // 16) * 16
    atoms = atom_orbitals.shape[0]
    chunks = 2 * mag // ROWS
    quarter = n // 4
    wide = 2 * mag
    assert offsets.shape[1] == n and n % 8 == 0 and mag % ROWS == 0
    sends = chunks
    pieces = norb // PIECE
    assert norb % PIECE == 0 and ROWS == 16
    f32, bf16 = jnp.float32, jnp.bfloat16
    tile = (ROWS, wide)
    dma = pltpu.SemaphoreType.DMA
    on_smem = (3, 4, 5, 7, 8)
    staged = [
        (pltpu.SMEM if i in on_smem else pltpu.VMEM)(arg.shape, arg.dtype)
        for i, arg in enumerate(args)
    ]
    return pl.pallas_call(
        functools.partial(kernel, n),
        out_shape=jax.ShapeDtypeStruct((1, atoms, atoms), f32),
        in_specs=[pl.BlockSpec(memory_space=pltpu.HBM)] * len(args),
        out_specs=pl.BlockSpec(memory_space=pltpu.VMEM),
        scratch_shapes=staged
        + [
            pltpu.VMEM((2, mag, 2 * norb), f32),
            pltpu.VMEM((wide, 2 * PIECE), bf16),
            pltpu.VMEM((2, pieces, 2 * PIECE, wide), bf16),
            pltpu.VMEM((2, slots, norb), f32),
            pltpu.VMEM((2, slots, norb), f32),
            pltpu.VMEM((2, slots, norb), f32),
            pltpu.VMEM((mag * slots, wide), f32),
            pltpu.VMEM((mag * slots, wide), f32),
            pltpu.VMEM((8 * n, 8 * slots), bf16),
            pltpu.VMEM((pieces, ROWS * slots, 2 * PIECE), bf16),
            pltpu.VMEM((chunks, 2, 2, quarter) + tile, f32),
            pltpu.VMEM((chunks, quarter) + tile, f32),
            pltpu.VMEM((chunks,) + tile, f32),
            pltpu.VMEM((chunks, 2, quarter) + tile, f32),
            pltpu.VMEM((chunks, quarter) + tile, f32),
            pltpu.VMEM((chunks, quarter) + tile, f32),
            pltpu.VMEM((chunks, quarter - 1) + tile, f32),
            dma((len(args),)),
            dma((sends,)),
            dma((sends,)),
            dma((sends,)),
            dma((sends,)),
            dma((sends, quarter - 1)),
            dma((sends, quarter - 1)),
        ],
        compiler_params=pltpu.CompilerParams(
            collective_id=0, has_side_effects=True, vmem_limit_bytes=63 * 1024 * 1024
        ),
    )(*args)


def solution(mesh):
    placed = (
        P("ka", None, None, None),
        P("ka", None, None),
        P(None, "ka"),
        P("ka"),
        P("grp"),
        P("grp"),
        P(),
        P(),
        P(),
        P(),
    )
    return jax.shard_map(
        functools.partial(local, mesh.shape["ka"]),
        mesh=mesh,
        in_specs=placed,
        out_specs=P(("grp", "ka"), None, None),
        check_vma=False,
    )
```

```python
import functools

import jax
import jax.numpy as jnp
from jax import lax
from jax.experimental import pallas as pl
from jax.experimental.pallas import tpu as pltpu
from jax.sharding import PartitionSpec as P

inv_four_pi = 0.25 / 3.141592653589793
two_pi = 2.0 * 3.141592653589793

ROWS = 16
HIGH = lax.Precision.HIGHEST
PIECE = 128
ACROSS = (((1,), (1,)), ((), ()))


def wave(turns):
    def cosine(part):
        part = part - jnp.round(part)
        x = (0.25 - jnp.abs(part)) * two_pi
        u = x * x
        series = 1.0 / 6227020800.0
        for term in (-1.0 / 39916800.0, 1.0 / 362880.0, -1.0 / 5040.0, 1.0 / 120.0, -1.0 / 6.0):
            series = series * u + term
        return x + x * (u * series)

    turns = turns - jnp.round(turns)
    return cosine(turns), cosine(turns - 0.25)


def one_hot(condition):
    return jnp.where(condition, 1.0, 0.0).astype(jnp.bfloat16)


def iota(shape, axis):
    return lax.broadcasted_iota(jnp.int32, shape, axis)


def kernel(
    n,
    vec_hbm,
    lev_hbm,
    k_hbm,
    count_hbm,
    er_hbm,
    ei_hbm,
    off_hbm,
    orb_hbm,
    pos_hbm,
    split_hbm,
    out_ref,
    vec_ref,
    lev_ref,
    k_ref,
    count_ref,
    er_ref,
    ei_ref,
    off_ref,
    orb_ref,
    pos_ref,
    split_ref,
    vf,
    right,
    flipped,
    levels,
    fre,
    fim,
    ctab,
    stab,
    wbd,
    scaled,
    acc,
    acc2,
    acc3,
    recv1,
    send2,
    recv2,
    recv3,
    isem,
    ssem1,
    rsem1,
    ssem2,
    rsem2,
    ssem3,
    rsem3,
):
    fetches = [
        pltpu.make_async_copy(source, target, isem.at[i])
        for i, (source, target) in enumerate(
            [
                (vec_hbm, vec_ref),
                (lev_hbm, lev_ref),
                (er_hbm, er_ref),
                (ei_hbm, ei_ref),
                (k_hbm, k_ref),
                (orb_hbm, orb_ref),
                (pos_hbm, pos_ref),
                (off_hbm, off_ref),
                (count_hbm, count_ref),
                (split_hbm, split_ref),
            ]
        )
    ]
    for fetch in fetches:
        fetch.start()

    mag, norb = vec_ref.shape[2], vec_ref.shape[3] // 2
    kslot = lev_ref.shape[0]
    slots = levels.shape[1]
    atoms = orb_ref.shape[0]
    blocks = mag // ROWS
    pieces = norb // PIECE
    quarter, eighth = n // 4, n // 8
    wide = 2 * mag

    me = lax.axis_index("ka")
    b0, b1, q = lax.rem(me, 2), lax.rem(me // 2, 2), me // 4
    mate0 = {"ka": me + 1 - 2 * b0}
    mate1 = {"ka": me + 2 - 4 * b1}

    def peer(k):
        return lax.rem(q + k, quarter)

    def peer_id(k):
        return {"ka": peer(k) * 4 + b1 * 2 + b0}

    barrier = pltpu.get_barrier_semaphore()
    for other in [mate0, mate1] + [peer_id(k) for k in range(1, quarter)]:
        pl.semaphore_signal(
            barrier, inc=1, device_id=other, device_id_type=pl.DeviceIdType.MESH
        )
    for fetch in fetches:
        fetch.wait()

    for s in range(kslot):
        row = lev_ref[s].astype(jnp.float32)
        levels[0, s : s + 1, :] = row[0:1]
        levels[1, s : s + 1, :] = row[1:2]
    er, ei = er_ref[0], ei_ref[0]

    def prepare(spin, carry):
        levels[spin, kslot:, :] = jnp.zeros((slots - kslot, norb), jnp.float32)
        vectors = vec_ref[0, spin]
        vf[spin] = vectors.astype(jnp.float32)
        for t in range(pieces):
            re_part = vectors[:, t * PIECE : (t + 1) * PIECE]
            im_part = vectors[:, norb + t * PIECE : norb + (t + 1) * PIECE]
            right[:mag, :PIECE] = re_part
            right[:mag, PIECE:] = im_part
            right[mag:, :PIECE] = -im_part
            right[mag:, PIECE:] = re_part
            flipped[spin, t] = right[...].T
        shift = er - levels[spin]
        denom = shift * shift + ei * ei
        inverse = 1.0 / denom
        fre[spin] = shift * inverse
        fim[spin] = -ei * inverse
        return carry

    lax.fori_loop(0, 2, prepare, 0)

    lane = iota((1, wide), 1)
    lane = jnp.where(lane >= mag, lane - mag, lane)
    down_rows = iota((mag, 1), 0)
    id_row = jnp.zeros((1, wide), jnp.int32)
    id_col = jnp.zeros((mag, 1), jnp.int32)
    end = jnp.int32(0)
    for i in range(atoms):
        end = end + orb_ref[i]
        id_row = id_row + jnp.where(lane >= end, 1, 0)
        id_col = id_col + jnp.where(down_rows >= end, 1, 0)

    coords = k_ref[...]
    eye = one_hot(iota((slots, kslot), 0) == iota((slots, kslot), 1))
    k_cols = lax.dot_general(eye, coords, ACROSS, preferred_element_type=jnp.float32)
    kpos = jnp.zeros((slots, wide), jnp.float32)
    for x in range(3):
        site = jnp.zeros((1, wide), jnp.float32)
        for i in range(atoms):
            site = jnp.where(id_row == i, pos_ref[x, i], site)
        kpos = kpos + k_cols[:, x : x + 1] * site
    cos_c, sin_c = wave(kpos)
    sign = jnp.where(iota((1, wide), 1) < mag, -1.0, 1.0)
    cos_s, sin_s = cos_c * sign, sin_c * sign
    deep = 8 * slots

    def gauge(h, carry):
        cos_r = pltpu.roll(cos_c, wide - 8 * h, 1)
        sin_r = pltpu.roll(sin_c, wide - 8 * h, 1)
        for j in range(8):
            cos_a, sin_a = cos_r[:, j : j + 1], sin_r[:, j : j + 1]
            here = pl.ds(pl.multiple_of(h * deep + j * slots, slots), slots)
            ctab[here, :] = cos_c * cos_a + sin_c * sin_a
            stab[here, :] = sin_s * cos_a - cos_s * sin_a
        return carry

    lax.fori_loop(0, mag // 8, gauge, 0)

    half = n // 2
    ordered = iota((half, n), 0)
    wanted = (
        lax.rem(ordered, eighth) * 4
        + lax.rem(ordered // eighth, 2) * 2
        + ordered // quarter
    )
    pick = one_hot(wanted == iota((half, n), 1))
    lattice = off_ref[...].astype(jnp.float32).astype(jnp.bfloat16)
    off_cols = lax.dot_general(pick, lattice, ACROSS, preferred_element_type=jnp.float32)
    spread = one_hot(iota((kslot, slots), 0) == iota((kslot, slots), 1))
    k_rows = jnp.dot(coords, spread, preferred_element_type=jnp.float32)
    turns = jnp.zeros((half, slots), jnp.float32)
    for x in range(3):
        turns = turns + off_cols[:, x : x + 1] * k_rows[x : x + 1, :]
    cos_t, sin_t = wave(turns)
    count = jnp.full((1, slots), count_ref[0], jnp.int32)
    weight = (1.0 / count.astype(jnp.float32)).astype(jnp.bfloat16).astype(jnp.float32)
    weight = jnp.where(iota((1, slots), 1) < count, weight, 0.0)
    table = jnp.concatenate([cos_t * weight, sin_t * weight], 0).astype(jnp.bfloat16)
    rows_of = one_hot(iota((8 * n, n), 0) // 8 == iota((8 * n, n), 1))
    tall = jnp.dot(rows_of, table, preferred_element_type=jnp.float32).astype(jnp.bfloat16)
    lanes_of = one_hot(iota((slots, deep), 0) == lax.rem(iota((slots, deep), 1), slots))
    full = jnp.dot(tall, lanes_of, preferred_element_type=jnp.float32)
    own = lax.rem(iota((8 * n, deep), 0), 8) == iota((8 * n, deep), 1) // slots
    wbd[...] = jnp.where(own, full, 0.0).astype(jnp.bfloat16)

    same = id_col == id_row[:, :mag]
    split = split_ref[...]
    splitting = jnp.where(same, 0.5 * (split + split.T), 0.0)
    member_rows = jnp.where(iota((atoms, mag), 0) == id_row[:, :mag], 1.0, 0.0)
    member_cols = jnp.where(id_col == iota((mag, atoms), 1), 1.0, 0.0)

    def compute(c):
        spin, start = c // blocks, lax.rem(c, blocks) * ROWS
        bare = None
        for t in range(pieces):
            at = slice(t * PIECE, (t + 1) * PIECE)
            f_re, f_im = fre[spin, :, at], fim[spin, :, at]
            mirror = slice(norb + t * PIECE, norb + (t + 1) * PIECE)
            these = pl.ds(pl.multiple_of(start, ROWS), ROWS)
            rows_re, rows_im = vf[spin, these, at], vf[spin, these, mirror]
            for j in range(ROWS):
                v_re, v_im = rows_re[j : j + 1], rows_im[j : j + 1]
                band = slice(j * slots, (j + 1) * slots)
                scaled[t, band, :PIECE] = (v_re * f_re - v_im * f_im).astype(jnp.bfloat16)
                scaled[t, band, PIECE:] = (v_re * f_im + v_im * f_re).astype(jnp.bfloat16)
            part = jnp.dot(scaled[t], flipped[spin, t], preferred_element_type=jnp.float32)
            bare = part if t == 0 else bare + part
        here = pl.ds(pl.multiple_of(start * slots, ROWS * slots), ROWS * slots)
        green = bare * ctab[here, :] + pltpu.roll(bare, mag, 1) * stab[here, :]
        green = green.astype(jnp.bfloat16)
        side = jnp.concatenate([green[:deep], green[deep:]], 1)
        mixed = jnp.dot(wbd[...], side, preferred_element_type=jnp.float32)
        sense = jnp.where(spin == 0, 1.0, -1.0) * -sign
        for part in range(ROWS // 8):
            half_mixed = mixed[:, part * wide : (part + 1) * wide]
            even = half_mixed[: 4 * n].reshape(2, 2, eighth, 8, wide)
            odd = pltpu.roll(half_mixed[4 * n :], mag, 1) * sense
            odd = odd.reshape(2, 2, eighth, 8, wide)
            rows = slice(part * 8, part * 8 + 8)
            acc[c, :, :, :eighth, rows, :] = even + odd
            acc[c, :, :, eighth:, rows, :] = even - odd

    def copy1(c):
        return pltpu.make_async_remote_copy(
            src_ref=acc.at[c, 1 - b0],
            dst_ref=recv1.at[c],
            send_sem=ssem1.at[c],
            recv_sem=rsem1.at[c],
            device_id=mate0,
            device_id_type=pl.DeviceIdType.MESH,
        )

    def copy2(c):
        return pltpu.make_async_remote_copy(
            src_ref=send2.at[c],
            dst_ref=recv2.at[c],
            send_sem=ssem2.at[c],
            recv_sem=rsem2.at[c],
            device_id=mate1,
            device_id_type=pl.DeviceIdType.MESH,
        )

    def copy3(c, k):
        return pltpu.make_async_remote_copy(
            src_ref=acc2.at[c, peer(k)],
            dst_ref=recv3.at[c, k - 1],
            send_sem=ssem3.at[c, k - 1],
            recv_sem=rsem3.at[c, k - 1],
            device_id=peer_id(k),
            device_id_type=pl.DeviceIdType.MESH,
        )

    def stage1(c):
        copy1(c).start()

    def stage2(c):
        copy1(c).wait()
        send2[c] = acc[c, b0, 1 - b1] + recv1[c, 1 - b1]
        copy2(c).start()
        acc2[c] = acc[c, b0, b1] + recv1[c, b1]

    def stage3(c):
        copy2(c).wait()
        acc2[c] = acc2[c] + recv2[c]
        for k in range(1, quarter):
            copy3(c, k).start()
        acc3[c] = acc2[c, q]

    def stage4(c, carry):
        for k in range(1, quarter):
            copy3(c, k).wait()
        total = acc3[c]
        for k in range(1, quarter):
            total = total + recv3[c, k - 1]
        acc3[c] = total
        return carry

    chunks = 2 * blocks
    pl.semaphore_wait(barrier, quarter + 1)

    def step(c, carry):
        compute(c)
        stage1(c)

        @pl.when(c >= 2)
        def _():
            stage2(c - 2)

        @pl.when(c >= 4)
        def _():
            stage3(c - 4)

        return carry

    lax.fori_loop(0, chunks, step, 0)
    stage2(chunks - 2)
    stage3(chunks - 4)
    stage3(chunks - 3)
    stage2(chunks - 1)
    stage3(chunks - 2)
    lax.fori_loop(0, blocks, stage4, 0)
    up = acc3[:blocks].reshape(mag, wide)
    left = jnp.dot(splitting, up, precision=HIGH, preferred_element_type=jnp.float32)
    stage3(chunks - 1)
    lax.fori_loop(blocks, chunks, stage4, 0)

    down = acc3[blocks:].reshape(mag, wide)
    turned = jnp.dot(down.T, splitting, precision=HIGH, preferred_element_type=jnp.float32)
    im_part = left[:, :mag] * turned[mag:] + left[:, mag:] * turned[:mag]
    by_atom = jnp.dot(member_rows, im_part, precision=HIGH, preferred_element_type=jnp.float32)
    pairs = jnp.dot(by_atom, member_cols, precision=HIGH, preferred_element_type=jnp.float32)
    out_ref[0] = -inv_four_pi * pairs


def local(n, *args):
    eigvecs, eigvals, offsets, atom_orbitals = args[0], args[1], args[6], args[7]
    mag, norb = eigvecs.shape[2], eigvals.shape[2]
    slots = -(-eigvals.shape[0] // 16) * 16
    atoms = atom_orbitals.shape[0]
    chunks = 2 * mag // ROWS
    quarter = n // 4
    wide = 2 * mag
    assert offsets.shape[1] == n and n % 8 == 0 and mag % ROWS == 0
    sends = chunks
    pieces = norb // PIECE
    assert norb % PIECE == 0 and ROWS == 16
    f32, bf16 = jnp.float32, jnp.bfloat16
    tile = (ROWS, wide)
    dma = pltpu.SemaphoreType.DMA
    on_smem = (3, 4, 5, 7, 8)
    staged = [
        (pltpu.SMEM if i in on_smem else pltpu.VMEM)(arg.shape, arg.dtype)
        for i, arg in enumerate(args)
    ]
    return pl.pallas_call(
        functools.partial(kernel, n),
        out_shape=jax.ShapeDtypeStruct((1, atoms, atoms), f32),
        in_specs=[pl.BlockSpec(memory_space=pltpu.HBM)] * len(args),
        out_specs=pl.BlockSpec(memory_space=pltpu.VMEM),
        scratch_shapes=staged
        + [
            pltpu.VMEM((2, mag, 2 * norb), f32),
            pltpu.VMEM((wide, 2 * PIECE), bf16),
            pltpu.VMEM((2, pieces, 2 * PIECE, wide), bf16),
            pltpu.VMEM((2, slots, norb), f32),
            pltpu.VMEM((2, slots, norb), f32),
            pltpu.VMEM((2, slots, norb), f32),
            pltpu.VMEM((mag * slots, wide), f32),
            pltpu.VMEM((mag * slots, wide), f32),
            pltpu.VMEM((8 * n, 8 * slots), bf16),
            pltpu.VMEM((pieces, ROWS * slots, 2 * PIECE), bf16),
            pltpu.VMEM((chunks, 2, 2, quarter) + tile, f32),
            pltpu.VMEM((chunks, quarter) + tile, f32),
            pltpu.VMEM((chunks,) + tile, f32),
            pltpu.VMEM((chunks, 2, quarter) + tile, f32),
            pltpu.VMEM((chunks, quarter) + tile, f32),
            pltpu.VMEM((chunks, quarter) + tile, f32),
            pltpu.VMEM((chunks, quarter - 1) + tile, f32),
            dma((len(args),)),
            dma((sends,)),
            dma((sends,)),
            dma((sends,)),
            dma((sends,)),
            dma((sends, quarter - 1)),
            dma((sends, quarter - 1)),
        ],
        compiler_params=pltpu.CompilerParams(
            collective_id=0, has_side_effects=True, vmem_limit_bytes=63 * 1024 * 1024
        ),
    )(*args)


def solution(mesh):
    placed = (
        P("ka", None, None, None),
        P("ka", None, None),
        P(None, "ka"),
        P("ka"),
        P("grp"),
        P("grp"),
        P(),
        P(),
        P(),
        P(),
    )
    return jax.shard_map(
        functools.partial(local, mesh.shape["ka"]),
        mesh=mesh,
        in_specs=placed,
        out_specs=P(("grp", "ka"), None, None),
        check_vma=False,
    )
```

```python
import functools

import jax
import jax.numpy as jnp
from jax import lax
from jax.experimental import pallas as pl
from jax.experimental.pallas import tpu as pltpu
from jax.sharding import PartitionSpec as P

inv_four_pi = 0.25 / 3.141592653589793
two_pi = 2.0 * 3.141592653589793

ROWS = 16
HIGH = lax.Precision.HIGHEST
PIECE = 128
ACROSS = (((1,), (1,)), ((), ()))


def wave(turns):
    def cosine(part):
        part = part - jnp.round(part)
        x = (0.25 - jnp.abs(part)) * two_pi
        u = x * x
        series = 1.0 / 6227020800.0
        for term in (-1.0 / 39916800.0, 1.0 / 362880.0, -1.0 / 5040.0, 1.0 / 120.0, -1.0 / 6.0):
            series = series * u + term
        return x + x * (u * series)

    turns = turns - jnp.round(turns)
    return cosine(turns), cosine(turns - 0.25)


def one_hot(condition):
    return jnp.where(condition, 1.0, 0.0).astype(jnp.bfloat16)


def iota(shape, axis):
    return lax.broadcasted_iota(jnp.int32, shape, axis)


def kernel(
    n,
    vec_hbm,
    lev_hbm,
    k_hbm,
    count_hbm,
    er_hbm,
    ei_hbm,
    off_hbm,
    orb_hbm,
    pos_hbm,
    split_hbm,
    out_ref,
    vec_ref,
    lev_ref,
    k_ref,
    count_ref,
    er_ref,
    ei_ref,
    off_ref,
    orb_ref,
    pos_ref,
    split_ref,
    vf,
    right,
    flipped,
    levels,
    fre,
    fim,
    ctab,
    stab,
    wbd,
    scaled,
    acc,
    acc2,
    acc3,
    recv1,
    send2,
    recv2,
    recv3,
    isem,
    ssem1,
    rsem1,
    ssem2,
    rsem2,
    ssem3,
    rsem3,
):
    fetches = [
        pltpu.make_async_copy(source, target, isem.at[i])
        for i, (source, target) in enumerate(
            [
                (vec_hbm, vec_ref),
                (lev_hbm, lev_ref),
                (er_hbm, er_ref),
                (ei_hbm, ei_ref),
                (k_hbm, k_ref),
                (orb_hbm, orb_ref),
                (pos_hbm, pos_ref),
                (off_hbm, off_ref),
                (count_hbm, count_ref),
                (split_hbm, split_ref),
            ]
        )
    ]
    for fetch in fetches:
        fetch.start()

    mag, norb = vec_ref.shape[2], vec_ref.shape[3] // 2
    kslot = lev_ref.shape[0]
    slots = levels.shape[1]
    atoms = orb_ref.shape[0]
    blocks = mag // ROWS
    pieces = norb // PIECE
    quarter, eighth = n // 4, n // 8
    wide = 2 * mag

    me = lax.axis_index("ka")
    b0, b1, q = lax.rem(me, 2), lax.rem(me // 2, 2), me // 4
    mate0 = {"ka": me + 1 - 2 * b0}
    mate1 = {"ka": me + 2 - 4 * b1}

    def peer(k):
        return lax.rem(q + k, quarter)

    def peer_id(k):
        return {"ka": peer(k) * 4 + b1 * 2 + b0}

    barrier = pltpu.get_barrier_semaphore()
    for other in [mate0, mate1] + [peer_id(k) for k in range(1, quarter)]:
        pl.semaphore_signal(
            barrier, inc=1, device_id=other, device_id_type=pl.DeviceIdType.MESH
        )
    for fetch in fetches:
        fetch.wait()

    for s in range(kslot):
        row = lev_ref[s].astype(jnp.float32)
        levels[0, s : s + 1, :] = row[0:1]
        levels[1, s : s + 1, :] = row[1:2]
    er, ei = er_ref[0], ei_ref[0]

    def prepare(spin, carry):
        levels[spin, kslot:, :] = jnp.zeros((slots - kslot, norb), jnp.float32)
        vectors = vec_ref[0, spin]
        vf[spin] = vectors.astype(jnp.float32)
        for t in range(pieces):
            re_part = vectors[:, t * PIECE : (t + 1) * PIECE]
            im_part = vectors[:, norb + t * PIECE : norb + (t + 1) * PIECE]
            right[:mag, :PIECE] = re_part
            right[:mag, PIECE:] = im_part
            right[mag:, :PIECE] = -im_part
            right[mag:, PIECE:] = re_part
            flipped[spin, t] = right[...].T
        shift = er - levels[spin]
        denom = shift * shift + ei * ei
        inverse = 1.0 / denom
        fre[spin] = shift * inverse
        fim[spin] = -ei * inverse
        return carry

    lax.fori_loop(0, 2, prepare, 0)

    lane = iota((1, wide), 1)
    lane = jnp.where(lane >= mag, lane - mag, lane)
    down_rows = iota((mag, 1), 0)
    id_row = jnp.zeros((1, wide), jnp.int32)
    id_col = jnp.zeros((mag, 1), jnp.int32)
    end = jnp.int32(0)
    for i in range(atoms):
        end = end + orb_ref[i]
        id_row = id_row + jnp.where(lane >= end, 1, 0)
        id_col = id_col + jnp.where(down_rows >= end, 1, 0)

    coords = k_ref[...]
    eye = one_hot(iota((slots, kslot), 0) == iota((slots, kslot), 1))
    k_cols = lax.dot_general(eye, coords, ACROSS, preferred_element_type=jnp.float32)
    kpos = jnp.zeros((slots, wide), jnp.float32)
    for x in range(3):
        site = jnp.zeros((1, wide), jnp.float32)
        for i in range(atoms):
            site = jnp.where(id_row == i, pos_ref[x, i], site)
        kpos = kpos + k_cols[:, x : x + 1] * site
    cos_c, sin_c = wave(kpos)
    sign = jnp.where(iota((1, wide), 1) < mag, -1.0, 1.0)
    cos_s, sin_s = cos_c * sign, sin_c * sign
    deep = 8 * slots

    def gauge(h, carry):
        cos_r = pltpu.roll(cos_c, wide - 8 * h, 1)
        sin_r = pltpu.roll(sin_c, wide - 8 * h, 1)
        for j in range(8):
            cos_a, sin_a = cos_r[:, j : j + 1], sin_r[:, j : j + 1]
            here = pl.ds(pl.multiple_of(h * deep + j * slots, slots), slots)
            ctab[here, :] = cos_c * cos_a + sin_c * sin_a
            stab[here, :] = sin_s * cos_a - cos_s * sin_a
        return carry

    lax.fori_loop(0, mag // 8, gauge, 0)

    half = n // 2
    ordered = iota((half, n), 0)
    wanted = (
        lax.rem(ordered, eighth) * 4
        + lax.rem(ordered // eighth, 2) * 2
        + ordered // quarter
    )
    pick = one_hot(wanted == iota((half, n), 1))
    lattice = off_ref[...].astype(jnp.float32).astype(jnp.bfloat16)
    off_cols = lax.dot_general(pick, lattice, ACROSS, preferred_element_type=jnp.float32)
    spread = one_hot(iota((kslot, slots), 0) == iota((kslot, slots), 1))
    k_rows = jnp.dot(coords, spread, preferred_element_type=jnp.float32)
    turns = jnp.zeros((half, slots), jnp.float32)
    for x in range(3):
        turns = turns + off_cols[:, x : x + 1] * k_rows[x : x + 1, :]
    cos_t, sin_t = wave(turns)
    count = jnp.full((1, slots), count_ref[0], jnp.int32)
    weight = (1.0 / count.astype(jnp.float32)).astype(jnp.bfloat16).astype(jnp.float32)
    weight = jnp.where(iota((1, slots), 1) < count, weight, 0.0)
    table = jnp.concatenate([cos_t * weight, sin_t * weight], 0).astype(jnp.bfloat16)
    rows_of = one_hot(iota((8 * n, n), 0) // 8 == iota((8 * n, n), 1))
    tall = jnp.dot(rows_of, table, preferred_element_type=jnp.float32).astype(jnp.bfloat16)
    lanes_of = one_hot(iota((slots, deep), 0) == lax.rem(iota((slots, deep), 1), slots))
    full = jnp.dot(tall, lanes_of, preferred_element_type=jnp.float32)
    own = lax.rem(iota((8 * n, deep), 0), 8) == iota((8 * n, deep), 1) // slots
    wbd[...] = jnp.where(own, full, 0.0).astype(jnp.bfloat16)

    same = id_col == id_row[:, :mag]
    split = split_ref[...]
    splitting = jnp.where(same, 0.5 * (split + split.T), 0.0)
    member_rows = jnp.where(iota((atoms, mag), 0) == id_row[:, :mag], 1.0, 0.0)
    member_cols = jnp.where(id_col == iota((mag, atoms), 1), 1.0, 0.0)

    def compute(c):
        spin, start = c // blocks, lax.rem(c, blocks) * ROWS
        bare = None
        for t in range(pieces):
            at = slice(t * PIECE, (t + 1) * PIECE)
            f_re, f_im = fre[spin, :, at], fim[spin, :, at]
            mirror = slice(norb + t * PIECE, norb + (t + 1) * PIECE)
            these = pl.ds(pl.multiple_of(start, ROWS), ROWS)
            rows_re, rows_im = vf[spin, these, at], vf[spin, these, mirror]
            for j in range(ROWS):
                v_re, v_im = rows_re[j : j + 1], rows_im[j : j + 1]
                band = slice(j * slots, (j + 1) * slots)
                scaled[t, band, :PIECE] = (v_re * f_re - v_im * f_im).astype(jnp.bfloat16)
                scaled[t, band, PIECE:] = (v_re * f_im + v_im * f_re).astype(jnp.bfloat16)
            part = jnp.dot(scaled[t], flipped[spin, t], preferred_element_type=jnp.float32)
            bare = part if t == 0 else bare + part
        here = pl.ds(pl.multiple_of(start * slots, ROWS * slots), ROWS * slots)
        green = bare * ctab[here, :] + pltpu.roll(bare, mag, 1) * stab[here, :]
        green = green.astype(jnp.bfloat16)
        side = jnp.concatenate([green[:deep], green[deep:]], 1)
        mixed = jnp.dot(wbd[...], side, preferred_element_type=jnp.float32)
        sense = jnp.where(spin == 0, 1.0, -1.0) * -sign
        for part in range(ROWS // 8):
            half_mixed = mixed[:, part * wide : (part + 1) * wide]
            even = half_mixed[: 4 * n].reshape(2, 2, eighth, 8, wide)
            odd = pltpu.roll(half_mixed[4 * n :], mag, 1) * sense
            odd = odd.reshape(2, 2, eighth, 8, wide)
            rows = slice(part * 8, part * 8 + 8)
            acc[c, :, :, :eighth, rows, :] = even + odd
            acc[c, :, :, eighth:, rows, :] = even - odd

    def copy1(c):
        return pltpu.make_async_remote_copy(
            src_ref=acc.at[c, 1 - b0],
            dst_ref=recv1.at[c],
            send_sem=ssem1.at[c],
            recv_sem=rsem1.at[c],
            device_id=mate0,
            device_id_type=pl.DeviceIdType.MESH,
        )

    def copy2(c):
        return pltpu.make_async_remote_copy(
            src_ref=send2.at[c],
            dst_ref=recv2.at[c],
            send_sem=ssem2.at[c],
            recv_sem=rsem2.at[c],
            device_id=mate1,
            device_id_type=pl.DeviceIdType.MESH,
        )

    def copy3(c, k):
        return pltpu.make_async_remote_copy(
            src_ref=acc2.at[c, peer(k)],
            dst_ref=recv3.at[c, k - 1],
            send_sem=ssem3.at[c, k - 1],
            recv_sem=rsem3.at[c, k - 1],
            device_id=peer_id(k),
            device_id_type=pl.DeviceIdType.MESH,
        )

    def stage1(c):
        copy1(c).start()

    def stage2(c):
        copy1(c).wait()
        send2[c] = acc[c, b0, 1 - b1] + recv1[c, 1 - b1]
        copy2(c).start()
        acc2[c] = acc[c, b0, b1] + recv1[c, b1]

    def stage3(c):
        copy2(c).wait()
        acc2[c] = acc2[c] + recv2[c]
        for k in range(1, quarter):
            copy3(c, k).start()
        acc3[c] = acc2[c, q]

    def stage4(c, carry):
        for k in range(1, quarter):
            copy3(c, k).wait()
        total = acc3[c]
        for k in range(1, quarter):
            total = total + recv3[c, k - 1]
        acc3[c] = total
        return carry

    chunks = 2 * blocks
    pl.semaphore_wait(barrier, quarter + 1)

    def step(c, carry):
        compute(c)
        stage1(c)

        @pl.when(c >= 1)
        def _():
            stage2(c - 1)

        @pl.when(c >= 3)
        def _():
            stage3(c - 3)

        return carry

    lax.fori_loop(0, chunks, step, 0)
    stage3(chunks - 3)
    stage2(chunks - 1)
    stage3(chunks - 2)
    lax.fori_loop(0, blocks, stage4, 0)
    up = acc3[:blocks].reshape(mag, wide)
    left = jnp.dot(splitting, up, precision=HIGH, preferred_element_type=jnp.float32)
    stage3(chunks - 1)
    lax.fori_loop(blocks, chunks, stage4, 0)

    down = acc3[blocks:].reshape(mag, wide)
    turned = jnp.dot(down.T, splitting, precision=HIGH, preferred_element_type=jnp.float32)
    im_part = left[:, :mag] * turned[mag:] + left[:, mag:] * turned[:mag]
    by_atom = jnp.dot(member_rows, im_part, precision=HIGH, preferred_element_type=jnp.float32)
    pairs = jnp.dot(by_atom, member_cols, precision=HIGH, preferred_element_type=jnp.float32)
    out_ref[0] = -inv_four_pi * pairs


def local(n, *args):
    eigvecs, eigvals, offsets, atom_orbitals = args[0], args[1], args[6], args[7]
    mag, norb = eigvecs.shape[2], eigvals.shape[2]
    slots = -(-eigvals.shape[0] // 16) * 16
    atoms = atom_orbitals.shape[0]
    chunks = 2 * mag // ROWS
    quarter = n // 4
    wide = 2 * mag
    assert offsets.shape[1] == n and n % 8 == 0 and mag % ROWS == 0
    sends = chunks
    pieces = norb // PIECE
    assert norb % PIECE == 0 and ROWS == 16
    f32, bf16 = jnp.float32, jnp.bfloat16
    tile = (ROWS, wide)
    dma = pltpu.SemaphoreType.DMA
    on_smem = (3, 4, 5, 7, 8)
    staged = [
        (pltpu.SMEM if i in on_smem else pltpu.VMEM)(arg.shape, arg.dtype)
        for i, arg in enumerate(args)
    ]
    return pl.pallas_call(
        functools.partial(kernel, n),
        out_shape=jax.ShapeDtypeStruct((1, atoms, atoms), f32),
        in_specs=[pl.BlockSpec(memory_space=pltpu.HBM)] * len(args),
        out_specs=pl.BlockSpec(memory_space=pltpu.VMEM),
        scratch_shapes=staged
        + [
            pltpu.VMEM((2, mag, 2 * norb), f32),
            pltpu.VMEM((wide, 2 * PIECE), bf16),
            pltpu.VMEM((2, pieces, 2 * PIECE, wide), bf16),
            pltpu.VMEM((2, slots, norb), f32),
            pltpu.VMEM((2, slots, norb), f32),
            pltpu.VMEM((2, slots, norb), f32),
            pltpu.VMEM((mag * slots, wide), f32),
            pltpu.VMEM((mag * slots, wide), f32),
            pltpu.VMEM((8 * n, 8 * slots), bf16),
            pltpu.VMEM((pieces, ROWS * slots, 2 * PIECE), bf16),
            pltpu.VMEM((chunks, 2, 2, quarter) + tile, f32),
            pltpu.VMEM((chunks, quarter) + tile, f32),
            pltpu.VMEM((chunks,) + tile, f32),
            pltpu.VMEM((chunks, 2, quarter) + tile, f32),
            pltpu.VMEM((chunks, quarter) + tile, f32),
            pltpu.VMEM((chunks, quarter) + tile, f32),
            pltpu.VMEM((chunks, quarter - 1) + tile, f32),
            dma((len(args),)),
            dma((sends,)),
            dma((sends,)),
            dma((sends,)),
            dma((sends,)),
            dma((sends, quarter - 1)),
            dma((sends, quarter - 1)),
        ],
        compiler_params=pltpu.CompilerParams(
            collective_id=0, has_side_effects=True, vmem_limit_bytes=63 * 1024 * 1024
        ),
    )(*args)


def solution(mesh):
    placed = (
        P("ka", None, None, None),
        P("ka", None, None),
        P(None, "ka"),
        P("ka"),
        P("grp"),
        P("grp"),
        P(),
        P(),
        P(),
        P(),
    )
    return jax.shard_map(
        functools.partial(local, mesh.shape["ka"]),
        mesh=mesh,
        in_specs=placed,
        out_specs=P(("grp", "ka"), None, None),
        check_vma=False,
    )
```

```python
import functools

import jax
import jax.numpy as jnp
from jax import lax
from jax.experimental import pallas as pl
from jax.experimental.pallas import tpu as pltpu
from jax.sharding import PartitionSpec as P

inv_four_pi = 0.25 / 3.141592653589793
two_pi = 2.0 * 3.141592653589793

ROWS = 16
HIGH = lax.Precision.HIGHEST
PIECE = 128
ACROSS = (((1,), (1,)), ((), ()))


def wave(turns):
    def cosine(part):
        part = part - jnp.round(part)
        x = (0.25 - jnp.abs(part)) * two_pi
        u = x * x
        series = 1.0 / 6227020800.0
        for term in (-1.0 / 39916800.0, 1.0 / 362880.0, -1.0 / 5040.0, 1.0 / 120.0, -1.0 / 6.0):
            series = series * u + term
        return x + x * (u * series)

    turns = turns - jnp.round(turns)
    return cosine(turns), cosine(turns - 0.25)


def one_hot(condition):
    return jnp.where(condition, 1.0, 0.0).astype(jnp.bfloat16)


def iota(shape, axis):
    return lax.broadcasted_iota(jnp.int32, shape, axis)


def kernel(
    n,
    vec_hbm,
    lev_hbm,
    k_hbm,
    count_hbm,
    er_hbm,
    ei_hbm,
    off_hbm,
    orb_hbm,
    pos_hbm,
    split_hbm,
    out_ref,
    vec_ref,
    lev_ref,
    k_ref,
    count_ref,
    er_ref,
    ei_ref,
    off_ref,
    orb_ref,
    pos_ref,
    split_ref,
    vf,
    right,
    flipped,
    levels,
    fre,
    fim,
    ctab,
    stab,
    wbd,
    scaled,
    acc,
    acc2,
    acc3,
    recv1,
    send2,
    recv2,
    recv3,
    isem,
    ssem1,
    rsem1,
    ssem2,
    rsem2,
    ssem3,
    rsem3,
):
    fetches = [
        pltpu.make_async_copy(source, target, isem.at[i])
        for i, (source, target) in enumerate(
            [
                (vec_hbm, vec_ref),
                (lev_hbm, lev_ref),
                (er_hbm, er_ref),
                (ei_hbm, ei_ref),
                (k_hbm, k_ref),
                (orb_hbm, orb_ref),
                (pos_hbm, pos_ref),
                (off_hbm, off_ref),
                (count_hbm, count_ref),
                (split_hbm, split_ref),
            ]
        )
    ]
    for fetch in fetches:
        fetch.start()

    mag, norb = vec_ref.shape[2], vec_ref.shape[3] // 2
    kslot = lev_ref.shape[0]
    slots = levels.shape[1]
    atoms = orb_ref.shape[0]
    blocks = mag // ROWS
    pieces = norb // PIECE
    quarter, eighth = n // 4, n // 8
    wide = 2 * mag

    me = lax.axis_index("ka")
    b0, b1, q = lax.rem(me, 2), lax.rem(me // 2, 2), me // 4
    mate0 = {"ka": me + 1 - 2 * b0}
    mate1 = {"ka": me + 2 - 4 * b1}

    def peer(k):
        return lax.rem(q + k, quarter)

    def peer_id(k):
        return {"ka": peer(k) * 4 + b1 * 2 + b0}

    barrier = pltpu.get_barrier_semaphore()
    for other in [mate0, mate1] + [peer_id(k) for k in range(1, quarter)]:
        pl.semaphore_signal(
            barrier, inc=1, device_id=other, device_id_type=pl.DeviceIdType.MESH
        )
    for fetch in fetches:
        fetch.wait()

    for s in range(kslot):
        row = lev_ref[s].astype(jnp.float32)
        levels[0, s : s + 1, :] = row[0:1]
        levels[1, s : s + 1, :] = row[1:2]
    er, ei = er_ref[0], ei_ref[0]

    def prepare(spin, carry):
        levels[spin, kslot:, :] = jnp.zeros((slots - kslot, norb), jnp.float32)
        vectors = vec_ref[0, spin]
        vf[spin] = vectors.astype(jnp.float32)
        for t in range(pieces):
            re_part = vectors[:, t * PIECE : (t + 1) * PIECE]
            im_part = vectors[:, norb + t * PIECE : norb + (t + 1) * PIECE]
            right[:mag, :PIECE] = re_part
            right[:mag, PIECE:] = im_part
            right[mag:, :PIECE] = -im_part
            right[mag:, PIECE:] = re_part
            flipped[spin, t] = right[...].T
        shift = er - levels[spin]
        denom = shift * shift + ei * ei
        inverse = 1.0 / denom
        fre[spin] = shift * inverse
        fim[spin] = -ei * inverse
        return carry

    lax.fori_loop(0, 2, prepare, 0)

    lane = iota((1, wide), 1)
    lane = jnp.where(lane >= mag, lane - mag, lane)
    down_rows = iota((mag, 1), 0)
    id_row = jnp.zeros((1, wide), jnp.int32)
    id_col = jnp.zeros((mag, 1), jnp.int32)
    end = jnp.int32(0)
    for i in range(atoms):
        end = end + orb_ref[i]
        id_row = id_row + jnp.where(lane >= end, 1, 0)
        id_col = id_col + jnp.where(down_rows >= end, 1, 0)

    coords = k_ref[...]
    eye = one_hot(iota((slots, kslot), 0) == iota((slots, kslot), 1))
    k_cols = lax.dot_general(eye, coords, ACROSS, preferred_element_type=jnp.float32)
    kpos = jnp.zeros((slots, wide), jnp.float32)
    for x in range(3):
        site = jnp.zeros((1, wide), jnp.float32)
        for i in range(atoms):
            site = jnp.where(id_row == i, pos_ref[x, i], site)
        kpos = kpos + k_cols[:, x : x + 1] * site
    cos_c, sin_c = wave(kpos)
    sign = jnp.where(iota((1, wide), 1) < mag, -1.0, 1.0)
    cos_s, sin_s = cos_c * sign, sin_c * sign
    deep = 8 * slots

    def gauge(h, carry):
        cos_r = pltpu.roll(cos_c, wide - 8 * h, 1)
        sin_r = pltpu.roll(sin_c, wide - 8 * h, 1)
        for j in range(8):
            cos_a, sin_a = cos_r[:, j : j + 1], sin_r[:, j : j + 1]
            here = pl.ds(pl.multiple_of(h * deep + j * slots, slots), slots)
            ctab[here, :] = cos_c * cos_a + sin_c * sin_a
            stab[here, :] = sin_s * cos_a - cos_s * sin_a
        return carry

    lax.fori_loop(0, mag // 8, gauge, 0)

    half = n // 2
    ordered = iota((half, n), 0)
    wanted = (
        lax.rem(ordered, eighth) * 4
        + lax.rem(ordered // eighth, 2) * 2
        + ordered // quarter
    )
    pick = one_hot(wanted == iota((half, n), 1))
    lattice = off_ref[...].astype(jnp.float32).astype(jnp.bfloat16)
    off_cols = lax.dot_general(pick, lattice, ACROSS, preferred_element_type=jnp.float32)
    spread = one_hot(iota((kslot, slots), 0) == iota((kslot, slots), 1))
    k_rows = jnp.dot(coords, spread, preferred_element_type=jnp.float32)
    turns = jnp.zeros((half, slots), jnp.float32)
    for x in range(3):
        turns = turns + off_cols[:, x : x + 1] * k_rows[x : x + 1, :]
    cos_t, sin_t = wave(turns)
    count = jnp.full((1, slots), count_ref[0], jnp.int32)
    weight = (1.0 / count.astype(jnp.float32)).astype(jnp.bfloat16).astype(jnp.float32)
    weight = jnp.where(iota((1, slots), 1) < count, weight, 0.0)
    table = jnp.concatenate([cos_t * weight, sin_t * weight], 0).astype(jnp.bfloat16)
    rows_of = one_hot(iota((8 * n, n), 0) // 8 == iota((8 * n, n), 1))
    tall = jnp.dot(rows_of, table, preferred_element_type=jnp.float32).astype(jnp.bfloat16)
    lanes_of = one_hot(iota((slots, deep), 0) == lax.rem(iota((slots, deep), 1), slots))
    full = jnp.dot(tall, lanes_of, preferred_element_type=jnp.float32)
    own = lax.rem(iota((8 * n, deep), 0), 8) == iota((8 * n, deep), 1) // slots
    wbd[...] = jnp.where(own, full, 0.0).astype(jnp.bfloat16)

    same = id_col == id_row[:, :mag]
    split = split_ref[...]
    splitting = jnp.where(same, 0.5 * (split + split.T), 0.0)
    member_rows = jnp.where(iota((atoms, mag), 0) == id_row[:, :mag], 1.0, 0.0)
    member_cols = jnp.where(id_col == iota((mag, atoms), 1), 1.0, 0.0)

    def compute(c):
        spin, start = c // blocks, lax.rem(c, blocks) * ROWS
        bare = None
        for t in range(pieces):
            at = slice(t * PIECE, (t + 1) * PIECE)
            f_re, f_im = fre[spin, :, at], fim[spin, :, at]
            mirror = slice(norb + t * PIECE, norb + (t + 1) * PIECE)
            these = pl.ds(pl.multiple_of(start, ROWS), ROWS)
            rows_re, rows_im = vf[spin, these, at], vf[spin, these, mirror]
            for j in range(ROWS):
                v_re, v_im = rows_re[j : j + 1], rows_im[j : j + 1]
                band = slice(j * slots, (j + 1) * slots)
                scaled[t, band, :PIECE] = (v_re * f_re - v_im * f_im).astype(jnp.bfloat16)
                scaled[t, band, PIECE:] = (v_re * f_im + v_im * f_re).astype(jnp.bfloat16)
            part = jnp.dot(scaled[t], flipped[spin, t], preferred_element_type=jnp.float32)
            bare = part if t == 0 else bare + part
        here = pl.ds(pl.multiple_of(start * slots, ROWS * slots), ROWS * slots)
        green = bare * ctab[here, :] + pltpu.roll(bare, mag, 1) * stab[here, :]
        green = green.astype(jnp.bfloat16)
        side = jnp.concatenate([green[:deep], green[deep:]], 1)
        mixed = jnp.dot(wbd[...], side, preferred_element_type=jnp.float32)
        sense = jnp.where(spin == 0, 1.0, -1.0) * -sign
        for part in range(ROWS // 8):
            half_mixed = mixed[:, part * wide : (part + 1) * wide]
            even = half_mixed[: 4 * n].reshape(2, 2, eighth, 8, wide)
            odd = pltpu.roll(half_mixed[4 * n :], mag, 1) * sense
            odd = odd.reshape(2, 2, eighth, 8, wide)
            rows = slice(part * 8, part * 8 + 8)
            acc[c, :, :, :eighth, rows, :] = even + odd
            acc[c, :, :, eighth:, rows, :] = even - odd

    def copy1(c):
        return pltpu.make_async_remote_copy(
            src_ref=acc.at[c, 1 - b0],
            dst_ref=recv1.at[c],
            send_sem=ssem1.at[c],
            recv_sem=rsem1.at[c],
            device_id=mate0,
            device_id_type=pl.DeviceIdType.MESH,
        )

    def copy2(c):
        return pltpu.make_async_remote_copy(
            src_ref=send2.at[c],
            dst_ref=recv2.at[c],
            send_sem=ssem2.at[c],
            recv_sem=rsem2.at[c],
            device_id=mate1,
            device_id_type=pl.DeviceIdType.MESH,
        )

    def copy3(c, k):
        return pltpu.make_async_remote_copy(
            src_ref=acc2.at[c, peer(k)],
            dst_ref=recv3.at[c, k - 1],
            send_sem=ssem3.at[c, k - 1],
            recv_sem=rsem3.at[c, k - 1],
            device_id=peer_id(k),
            device_id_type=pl.DeviceIdType.MESH,
        )

    def stage1(c):
        copy1(c).start()

    def stage2(c):
        copy1(c).wait()
        send2[c] = acc[c, b0, 1 - b1] + recv1[c, 1 - b1]
        copy2(c).start()
        acc2[c] = acc[c, b0, b1] + recv1[c, b1]

    def stage3(c):
        copy2(c).wait()
        acc2[c] = acc2[c] + recv2[c]
        for k in range(1, quarter):
            copy3(c, k).start()
        acc3[c] = acc2[c, q]

    def stage4(c, carry):
        for k in range(1, quarter):
            copy3(c, k).wait()
        total = acc3[c]
        for k in range(1, quarter):
            total = total + recv3[c, k - 1]
        acc3[c] = total
        return carry

    chunks = 2 * blocks
    pl.semaphore_wait(barrier, quarter + 1)

    def step(c, carry):
        compute(c)
        stage1(c)

        @pl.when(c >= 1)
        def _():
            stage2(c - 1)

        @pl.when(c >= 4)
        def _():
            stage3(c - 4)

        return carry

    lax.fori_loop(0, chunks, step, 0)
    stage2(chunks - 1)
    stage3(chunks - 4)
    stage3(chunks - 3)
    stage3(chunks - 2)
    lax.fori_loop(0, blocks, stage4, 0)
    up = acc3[:blocks].reshape(mag, wide)
    left = jnp.dot(splitting, up, precision=HIGH, preferred_element_type=jnp.float32)
    stage3(chunks - 1)
    lax.fori_loop(blocks, chunks, stage4, 0)

    down = acc3[blocks:].reshape(mag, wide)
    turned = jnp.dot(down.T, splitting, precision=HIGH, preferred_element_type=jnp.float32)
    im_part = left[:, :mag] * turned[mag:] + left[:, mag:] * turned[:mag]
    by_atom = jnp.dot(member_rows, im_part, precision=HIGH, preferred_element_type=jnp.float32)
    pairs = jnp.dot(by_atom, member_cols, precision=HIGH, preferred_element_type=jnp.float32)
    out_ref[0] = -inv_four_pi * pairs


def local(n, *args):
    eigvecs, eigvals, offsets, atom_orbitals = args[0], args[1], args[6], args[7]
    mag, norb = eigvecs.shape[2], eigvals.shape[2]
    slots = -(-eigvals.shape[0] // 16) * 16
    atoms = atom_orbitals.shape[0]
    chunks = 2 * mag // ROWS
    quarter = n // 4
    wide = 2 * mag
    assert offsets.shape[1] == n and n % 8 == 0 and mag % ROWS == 0
    sends = chunks
    pieces = norb // PIECE
    assert norb % PIECE == 0 and ROWS == 16
    f32, bf16 = jnp.float32, jnp.bfloat16
    tile = (ROWS, wide)
    dma = pltpu.SemaphoreType.DMA
    on_smem = (3, 4, 5, 7, 8)
    staged = [
        (pltpu.SMEM if i in on_smem else pltpu.VMEM)(arg.shape, arg.dtype)
        for i, arg in enumerate(args)
    ]
    return pl.pallas_call(
        functools.partial(kernel, n),
        out_shape=jax.ShapeDtypeStruct((1, atoms, atoms), f32),
        in_specs=[pl.BlockSpec(memory_space=pltpu.HBM)] * len(args),
        out_specs=pl.BlockSpec(memory_space=pltpu.VMEM),
        scratch_shapes=staged
        + [
            pltpu.VMEM((2, mag, 2 * norb), f32),
            pltpu.VMEM((wide, 2 * PIECE), bf16),
            pltpu.VMEM((2, pieces, 2 * PIECE, wide), bf16),
            pltpu.VMEM((2, slots, norb), f32),
            pltpu.VMEM((2, slots, norb), f32),
            pltpu.VMEM((2, slots, norb), f32),
            pltpu.VMEM((mag * slots, wide), f32),
            pltpu.VMEM((mag * slots, wide), f32),
            pltpu.VMEM((8 * n, 8 * slots), bf16),
            pltpu.VMEM((pieces, ROWS * slots, 2 * PIECE), bf16),
            pltpu.VMEM((chunks, 2, 2, quarter) + tile, f32),
            pltpu.VMEM((chunks, quarter) + tile, f32),
            pltpu.VMEM((chunks,) + tile, f32),
            pltpu.VMEM((chunks, 2, quarter) + tile, f32),
            pltpu.VMEM((chunks, quarter) + tile, f32),
            pltpu.VMEM((chunks, quarter) + tile, f32),
            pltpu.VMEM((chunks, quarter - 1) + tile, f32),
            dma((len(args),)),
            dma((sends,)),
            dma((sends,)),
            dma((sends,)),
            dma((sends,)),
            dma((sends, quarter - 1)),
            dma((sends, quarter - 1)),
        ],
        compiler_params=pltpu.CompilerParams(
            collective_id=0, has_side_effects=True, vmem_limit_bytes=63 * 1024 * 1024
        ),
    )(*args)


def solution(mesh):
    placed = (
        P("ka", None, None, None),
        P("ka", None, None),
        P(None, "ka"),
        P("ka"),
        P("grp"),
        P("grp"),
        P(),
        P(),
        P(),
        P(),
    )
    return jax.shard_map(
        functools.partial(local, mesh.shape["ka"]),
        mesh=mesh,
        in_specs=placed,
        out_specs=P(("grp", "ka"), None, None),
        check_vma=False,
    )
```

```python
import functools

import jax
import jax.numpy as jnp
from jax import lax
from jax.experimental import pallas as pl
from jax.experimental.pallas import tpu as pltpu
from jax.sharding import PartitionSpec as P

inv_four_pi = 0.25 / 3.141592653589793
two_pi = 2.0 * 3.141592653589793

ROWS = 16
HIGH = lax.Precision.HIGHEST
PIECE = 128
ACROSS = (((1,), (1,)), ((), ()))


def wave(turns):
    def cosine(part):
        part = part - jnp.round(part)
        x = (0.25 - jnp.abs(part)) * two_pi
        u = x * x
        series = 1.0 / 6227020800.0
        for term in (-1.0 / 39916800.0, 1.0 / 362880.0, -1.0 / 5040.0, 1.0 / 120.0, -1.0 / 6.0):
            series = series * u + term
        return x + x * (u * series)

    turns = turns - jnp.round(turns)
    return cosine(turns), cosine(turns - 0.25)


def one_hot(condition):
    return jnp.where(condition, 1.0, 0.0).astype(jnp.bfloat16)


def iota(shape, axis):
    return lax.broadcasted_iota(jnp.int32, shape, axis)


def kernel(
    n,
    vec_hbm,
    lev_hbm,
    k_hbm,
    count_hbm,
    er_hbm,
    ei_hbm,
    off_hbm,
    orb_hbm,
    pos_hbm,
    split_hbm,
    out_ref,
    vec_ref,
    lev_ref,
    k_ref,
    count_ref,
    er_ref,
    ei_ref,
    off_ref,
    orb_ref,
    pos_ref,
    split_ref,
    vf,
    right,
    flipped,
    levels,
    fre,
    fim,
    ctab,
    stab,
    wbd,
    scaled,
    acc,
    acc2,
    acc3,
    recv1,
    send2,
    recv2,
    recv3,
    isem,
    ssem1,
    rsem1,
    ssem2,
    rsem2,
    ssem3,
    rsem3,
):
    fetches = [
        pltpu.make_async_copy(source, target, isem.at[i])
        for i, (source, target) in enumerate(
            [
                (vec_hbm, vec_ref),
                (lev_hbm, lev_ref),
                (er_hbm, er_ref),
                (ei_hbm, ei_ref),
                (k_hbm, k_ref),
                (orb_hbm, orb_ref),
                (pos_hbm, pos_ref),
                (off_hbm, off_ref),
                (count_hbm, count_ref),
                (split_hbm, split_ref),
            ]
        )
    ]
    for fetch in fetches:
        fetch.start()

    mag, norb = vec_ref.shape[2], vec_ref.shape[3] // 2
    kslot = lev_ref.shape[0]
    slots = levels.shape[1]
    atoms = orb_ref.shape[0]
    blocks = mag // ROWS
    pieces = norb // PIECE
    quarter, eighth = n // 4, n // 8
    wide = 2 * mag

    me = lax.axis_index("ka")
    b0, b1, q = lax.rem(me, 2), lax.rem(me // 2, 2), me // 4
    mate0 = {"ka": me + 1 - 2 * b0}
    mate1 = {"ka": me + 2 - 4 * b1}

    def peer(k):
        return lax.rem(q + k, quarter)

    def peer_id(k):
        return {"ka": peer(k) * 4 + b1 * 2 + b0}

    barrier = pltpu.get_barrier_semaphore()
    for other in [mate0, mate1] + [peer_id(k) for k in range(1, quarter)]:
        pl.semaphore_signal(
            barrier, inc=1, device_id=other, device_id_type=pl.DeviceIdType.MESH
        )
    for fetch in fetches:
        fetch.wait()

    for s in range(kslot):
        row = lev_ref[s].astype(jnp.float32)
        levels[0, s : s + 1, :] = row[0:1]
        levels[1, s : s + 1, :] = row[1:2]
    er, ei = er_ref[0], ei_ref[0]

    def prepare(spin, carry):
        levels[spin, kslot:, :] = jnp.zeros((slots - kslot, norb), jnp.float32)
        vectors = vec_ref[0, spin]
        vf[spin] = vectors.astype(jnp.float32)
        for t in range(pieces):
            re_part = vectors[:, t * PIECE : (t + 1) * PIECE]
            im_part = vectors[:, norb + t * PIECE : norb + (t + 1) * PIECE]
            right[:mag, :PIECE] = re_part
            right[:mag, PIECE:] = im_part
            right[mag:, :PIECE] = -im_part
            right[mag:, PIECE:] = re_part
            flipped[spin, t] = right[...].T
        shift = er - levels[spin]
        denom = shift * shift + ei * ei
        inverse = 1.0 / denom
        fre[spin] = shift * inverse
        fim[spin] = -ei * inverse
        return carry

    lax.fori_loop(0, 2, prepare, 0)

    lane = iota((1, wide), 1)
    lane = jnp.where(lane >= mag, lane - mag, lane)
    down_rows = iota((mag, 1), 0)
    id_row = jnp.zeros((1, wide), jnp.int32)
    id_col = jnp.zeros((mag, 1), jnp.int32)
    end = jnp.int32(0)
    for i in range(atoms):
        end = end + orb_ref[i]
        id_row = id_row + jnp.where(lane >= end, 1, 0)
        id_col = id_col + jnp.where(down_rows >= end, 1, 0)

    coords = k_ref[...]
    eye = one_hot(iota((slots, kslot), 0) == iota((slots, kslot), 1))
    k_cols = lax.dot_general(eye, coords, ACROSS, preferred_element_type=jnp.float32)
    kpos = jnp.zeros((slots, wide), jnp.float32)
    for x in range(3):
        site = jnp.zeros((1, wide), jnp.float32)
        for i in range(atoms):
            site = jnp.where(id_row == i, pos_ref[x, i], site)
        kpos = kpos + k_cols[:, x : x + 1] * site
    cos_c, sin_c = wave(kpos)
    sign = jnp.where(iota((1, wide), 1) < mag, -1.0, 1.0)
    cos_s, sin_s = cos_c * sign, sin_c * sign
    deep = 8 * slots

    def gauge(h, carry):
        cos_r = pltpu.roll(cos_c, wide - 8 * h, 1)
        sin_r = pltpu.roll(sin_c, wide - 8 * h, 1)
        for j in range(8):
            cos_a, sin_a = cos_r[:, j : j + 1], sin_r[:, j : j + 1]
            here = pl.ds(pl.multiple_of(h * deep + j * slots, slots), slots)
            ctab[here, :] = cos_c * cos_a + sin_c * sin_a
            stab[here, :] = sin_s * cos_a - cos_s * sin_a
        return carry

    lax.fori_loop(0, mag // 8, gauge, 0)

    half = n // 2
    ordered = iota((half, n), 0)
    wanted = (
        lax.rem(ordered, eighth) * 4
        + lax.rem(ordered // eighth, 2) * 2
        + ordered // quarter
    )
    pick = one_hot(wanted == iota((half, n), 1))
    lattice = off_ref[...].astype(jnp.float32).astype(jnp.bfloat16)
    off_cols = lax.dot_general(pick, lattice, ACROSS, preferred_element_type=jnp.float32)
    spread = one_hot(iota((kslot, slots), 0) == iota((kslot, slots), 1))
    k_rows = jnp.dot(coords, spread, preferred_element_type=jnp.float32)
    turns = jnp.zeros((half, slots), jnp.float32)
    for x in range(3):
        turns = turns + off_cols[:, x : x + 1] * k_rows[x : x + 1, :]
    cos_t, sin_t = wave(turns)
    count = jnp.full((1, slots), count_ref[0], jnp.int32)
    weight = (1.0 / count.astype(jnp.float32)).astype(jnp.bfloat16).astype(jnp.float32)
    weight = jnp.where(iota((1, slots), 1) < count, weight, 0.0)
    table = jnp.concatenate([cos_t * weight, sin_t * weight], 0).astype(jnp.bfloat16)
    rows_of = one_hot(iota((8 * n, n), 0) // 8 == iota((8 * n, n), 1))
    tall = jnp.dot(rows_of, table, preferred_element_type=jnp.float32).astype(jnp.bfloat16)
    lanes_of = one_hot(iota((slots, deep), 0) == lax.rem(iota((slots, deep), 1), slots))
    full = jnp.dot(tall, lanes_of, preferred_element_type=jnp.float32)
    own = lax.rem(iota((8 * n, deep), 0), 8) == iota((8 * n, deep), 1) // slots
    wbd[...] = jnp.where(own, full, 0.0).astype(jnp.bfloat16)

    same = id_col == id_row[:, :mag]
    split = split_ref[...]
    splitting = jnp.where(same, 0.5 * (split + split.T), 0.0)
    member_rows = jnp.where(iota((atoms, mag), 0) == id_row[:, :mag], 1.0, 0.0)
    member_cols = jnp.where(id_col == iota((mag, atoms), 1), 1.0, 0.0)

    def compute(c):
        spin, start = c // blocks, lax.rem(c, blocks) * ROWS
        bare = None
        for t in range(pieces):
            at = slice(t * PIECE, (t + 1) * PIECE)
            f_re, f_im = fre[spin, :, at], fim[spin, :, at]
            mirror = slice(norb + t * PIECE, norb + (t + 1) * PIECE)
            these = pl.ds(pl.multiple_of(start, ROWS), ROWS)
            rows_re, rows_im = vf[spin, these, at], vf[spin, these, mirror]
            for j in range(ROWS):
                v_re, v_im = rows_re[j : j + 1], rows_im[j : j + 1]
                band = slice(j * slots, (j + 1) * slots)
                scaled[t, band, :PIECE] = (v_re * f_re - v_im * f_im).astype(jnp.bfloat16)
                scaled[t, band, PIECE:] = (v_re * f_im + v_im * f_re).astype(jnp.bfloat16)
            part = jnp.dot(scaled[t], flipped[spin, t], preferred_element_type=jnp.float32)
            bare = part if t == 0 else bare + part
        here = pl.ds(pl.multiple_of(start * slots, ROWS * slots), ROWS * slots)
        green = bare * ctab[here, :] + pltpu.roll(bare, mag, 1) * stab[here, :]
        green = green.astype(jnp.bfloat16)
        side = jnp.concatenate([green[:deep], green[deep:]], 1)
        mixed = jnp.dot(wbd[...], side, preferred_element_type=jnp.float32)
        sense = jnp.where(spin == 0, 1.0, -1.0) * -sign
        for part in range(ROWS // 8):
            half_mixed = mixed[:, part * wide : (part + 1) * wide]
            even = half_mixed[: 4 * n].reshape(2, 2, eighth, 8, wide)
            odd = pltpu.roll(half_mixed[4 * n :], mag, 1) * sense
            odd = odd.reshape(2, 2, eighth, 8, wide)
            rows = slice(part * 8, part * 8 + 8)
            acc[c, :, :, :eighth, rows, :] = even + odd
            acc[c, :, :, eighth:, rows, :] = even - odd

    def copy1(c):
        return pltpu.make_async_remote_copy(
            src_ref=acc.at[c, 1 - b0],
            dst_ref=recv1.at[c],
            send_sem=ssem1.at[c],
            recv_sem=rsem1.at[c],
            device_id=mate0,
            device_id_type=pl.DeviceIdType.MESH,
        )

    def copy2(c):
        return pltpu.make_async_remote_copy(
            src_ref=send2.at[c],
            dst_ref=recv2.at[c],
            send_sem=ssem2.at[c],
            recv_sem=rsem2.at[c],
            device_id=mate1,
            device_id_type=pl.DeviceIdType.MESH,
        )

    def copy3(c, k):
        return pltpu.make_async_remote_copy(
            src_ref=acc2.at[c, peer(k)],
            dst_ref=recv3.at[c, k - 1],
            send_sem=ssem3.at[c, k - 1],
            recv_sem=rsem3.at[c, k - 1],
            device_id=peer_id(k),
            device_id_type=pl.DeviceIdType.MESH,
        )

    def stage1(c):
        copy1(c).start()

    def stage2(c):
        copy1(c).wait()
        send2[c] = acc[c, b0, 1 - b1] + recv1[c, 1 - b1]
        copy2(c).start()
        acc2[c] = acc[c, b0, b1] + recv1[c, b1]

    def stage3(c):
        copy2(c).wait()
        acc2[c] = acc2[c] + recv2[c]
        for k in range(1, quarter):
            copy3(c, k).start()
        acc3[c] = acc2[c, q]

    def stage4(c, carry):
        for k in range(1, quarter):
            copy3(c, k).wait()
        total = acc3[c]
        for k in range(1, quarter):
            total = total + recv3[c, k - 1]
        acc3[c] = total
        return carry

    chunks = 2 * blocks
    pl.semaphore_wait(barrier, quarter + 1)

    def step(c, carry):
        compute(c)
        stage1(c)

        @pl.when(c >= 1)
        def _():
            stage2(c - 1)

        @pl.when(c >= 5)
        def _():
            stage3(c - 5)

        return carry

    lax.fori_loop(0, chunks, step, 0)
    stage2(chunks - 1)
    stage3(chunks - 5)
    stage3(chunks - 4)
    stage3(chunks - 3)
    stage3(chunks - 2)
    lax.fori_loop(0, blocks, stage4, 0)
    up = acc3[:blocks].reshape(mag, wide)
    left = jnp.dot(splitting, up, precision=HIGH, preferred_element_type=jnp.float32)
    stage3(chunks - 1)
    lax.fori_loop(blocks, chunks, stage4, 0)

    down = acc3[blocks:].reshape(mag, wide)
    turned = jnp.dot(down.T, splitting, precision=HIGH, preferred_element_type=jnp.float32)
    im_part = left[:, :mag] * turned[mag:] + left[:, mag:] * turned[:mag]
    by_atom = jnp.dot(member_rows, im_part, precision=HIGH, preferred_element_type=jnp.float32)
    pairs = jnp.dot(by_atom, member_cols, precision=HIGH, preferred_element_type=jnp.float32)
    out_ref[0] = -inv_four_pi * pairs


def local(n, *args):
    eigvecs, eigvals, offsets, atom_orbitals = args[0], args[1], args[6], args[7]
    mag, norb = eigvecs.shape[2], eigvals.shape[2]
    slots = -(-eigvals.shape[0] // 16) * 16
    atoms = atom_orbitals.shape[0]
    chunks = 2 * mag // ROWS
    quarter = n // 4
    wide = 2 * mag
    assert offsets.shape[1] == n and n % 8 == 0 and mag % ROWS == 0
    sends = chunks
    pieces = norb // PIECE
    assert norb % PIECE == 0 and ROWS == 16
    f32, bf16 = jnp.float32, jnp.bfloat16
    tile = (ROWS, wide)
    dma = pltpu.SemaphoreType.DMA
    on_smem = (3, 4, 5, 7, 8)
    staged = [
        (pltpu.SMEM if i in on_smem else pltpu.VMEM)(arg.shape, arg.dtype)
        for i, arg in enumerate(args)
    ]
    return pl.pallas_call(
        functools.partial(kernel, n),
        out_shape=jax.ShapeDtypeStruct((1, atoms, atoms), f32),
        in_specs=[pl.BlockSpec(memory_space=pltpu.HBM)] * len(args),
        out_specs=pl.BlockSpec(memory_space=pltpu.VMEM),
        scratch_shapes=staged
        + [
            pltpu.VMEM((2, mag, 2 * norb), f32),
            pltpu.VMEM((wide, 2 * PIECE), bf16),
            pltpu.VMEM((2, pieces, 2 * PIECE, wide), bf16),
            pltpu.VMEM((2, slots, norb), f32),
            pltpu.VMEM((2, slots, norb), f32),
            pltpu.VMEM((2, slots, norb), f32),
            pltpu.VMEM((mag * slots, wide), f32),
            pltpu.VMEM((mag * slots, wide), f32),
            pltpu.VMEM((8 * n, 8 * slots), bf16),
            pltpu.VMEM((pieces, ROWS * slots, 2 * PIECE), bf16),
            pltpu.VMEM((chunks, 2, 2, quarter) + tile, f32),
            pltpu.VMEM((chunks, quarter) + tile, f32),
            pltpu.VMEM((chunks,) + tile, f32),
            pltpu.VMEM((chunks, 2, quarter) + tile, f32),
            pltpu.VMEM((chunks, quarter) + tile, f32),
            pltpu.VMEM((chunks, quarter) + tile, f32),
            pltpu.VMEM((chunks, quarter - 1) + tile, f32),
            dma((len(args),)),
            dma((sends,)),
            dma((sends,)),
            dma((sends,)),
            dma((sends,)),
            dma((sends, quarter - 1)),
            dma((sends, quarter - 1)),
        ],
        compiler_params=pltpu.CompilerParams(
            collective_id=0, has_side_effects=True, vmem_limit_bytes=63 * 1024 * 1024
        ),
    )(*args)


def solution(mesh):
    placed = (
        P("ka", None, None, None),
        P("ka", None, None),
        P(None, "ka"),
        P("ka"),
        P("grp"),
        P("grp"),
        P(),
        P(),
        P(),
        P(),
    )
    return jax.shard_map(
        functools.partial(local, mesh.shape["ka"]),
        mesh=mesh,
        in_specs=placed,
        out_specs=P(("grp", "ka"), None, None),
        check_vma=False,
    )
```
